256 devices in a mesh: expert: 32 (over z, x), dp: 8 (over y, core).
Axes of the slice: x: 4, y: 4, z: 8, core: 2. Of those that a mesh axis runs over, the one named last changes fastest.
Arguments:
- tokens: bfloat16 [32768, 2048], P(('expert', 'dp')), may hold values from -6 to 6
- routes: int32 [32768, 8], P(('expert', 'dp')), may hold values from 0 to 255, all different within a row; in each aligned block of 128 rows (0 to 127, 128 to 255, ...) at most 8 rows name the same one
- gates: float32 [32768, 8], P(('expert', 'dp')), may hold values from 0.1 to 1
- cotangent: bfloat16 [32768, 2048], P(('expert', 'dp')), may hold values from -6 to 6
- w_up: bfloat16 [256, 2048, 128], P('expert'), may hold values from -0.125 to 0.125
- w_down: bfloat16 [256, 128, 2048], P('expert'), may hold values from -0.5 to 0.5
Outputs:
- mixed: bfloat16 [32768, 2048], P(('expert', 'dp'))
- token_grad: bfloat16 [32768, 2048], P(('expert', 'dp'))
- grad_up: bfloat16 [256, 2048, 128], P('expert', 'dp')
- grad_down: bfloat16 [256, 128, 2048], P('expert', None, 'dp')
The draws below stay inside these ranges and needn't reach their ends.
Inputs may be any that keep to these rules, and one draw needn't show every extreme that they name: `routes`: each row names 8 different experts; within the rows of one device no expert is named more than min(8, 128) times, and some expert is named exactly that often.
All inputs are finite; a program needn't handle non-finite values.
Results may differ from the reference program's by a relative error of at most 0.013.
Values may be sent and summed in bfloat16 or wider, within the bound.
No kernel may reach another device: no remote copies, remote signals or barrier semaphores. Data moves between devices by JAX's collectives and lax.ppermute only.
A program may use at most 128 MiB of HBM per device.

```python
import math
import jax
import jax.numpy as jnp
import numpy as np
from jax import lax

D = 2048
F = 128
TOP = 8
TOK_DEV = 128
EXPERTS = 256
CAP = 4
TOKENS = 32768
N_EXPERT = 32
N_DP = 8


def level_of(own_key, extent, split, smallest, largest):
    def one(position, blocks):
        steps = jax.random.uniform(jax.random.fold_in(jax.random.fold_in(own_key, 6), position), (blocks,), jnp.float32, smallest / len(split), largest / len(split))
        return jnp.repeat(jnp.exp(steps), extent[position] // blocks).reshape((-1,) + (1,) * (len(extent) - position - 1))

    factor_of = one(*split[0])
    for cut in split[1:]:
        factor_of = factor_of * one(*cut)
    return factor_of


def shared_out(own_key, own, number, rows, count, top, bound, skew):
    order = jax.random.permutation(own_key, count)
    crowded, ordinary = portions_of(count, rows * top, bound, skew, True), portions_of(count, rows * top, bound, skew, False)
    places = jnp.arange(count)

    def named(sizes, turn):
        used = int((sizes > 0).sum())
        fixed = max(1, used // 4)
        moved = fixed + (places - fixed + turn * (used - fixed)) % max(1, count - fixed)
        return jnp.zeros((count,), jnp.int32).at[order[jnp.where(places < fixed, places, moved)]].set(jnp.asarray(sizes, jnp.int32))

    sizes = jnp.where(number % 4 == 0, named(crowded, number // 4), named(ordinary, number - number // 4 - 1))
    mixed = jax.random.permutation(jax.random.fold_in(own, 3), count)
    giver, taker = mixed[0:count // 2 * 2:2], mixed[1:count // 2 * 2:2]
    margin = jnp.minimum(sizes[giver] - 1, bound - sizes[taker]) // 2
    margin = jnp.where((giver == order[0]) | (taker == order[0]) | (sizes[taker] == 0), 0, jnp.maximum(margin, 0))
    moved = jax.random.randint(jax.random.fold_in(own, 4), (count // 2,), 0, 1 << 20) % (margin + 1)
    sizes = sizes.at[giver].add(-moved).at[taker].add(moved)
    members = jnp.searchsorted(jnp.cumsum(sizes), jnp.arange(rows * top), side="right").astype(jnp.int32)
    grid = members.reshape(top, rows).T
    grid = grid[jax.random.permutation(jax.random.fold_in(own, 1), rows)]
    turn = jax.random.randint(jax.random.fold_in(own, 2), (rows, 1), 0, top)
    return jnp.take_along_axis(grid, (jnp.arange(top)[None, :] + turn) % top, axis=1)


def portions_of(count, total, bound, lean, full):
    loads = [(1 << 20) // math.isqrt(rank ** lean) + 1 for rank in range(1, count + 1)]
    largest = bound if full else min(bound, max(-(-total // count), total * loads[0] // sum(loads)))
    least = 1 if total - largest >= count - 1 else 0
    counts, surplus = [largest] + [least] * (count - 1), total - largest - least * (count - 1)
    while surplus > 0:
        movable = [i for i in range(1, count) if counts[i] < largest] or [i for i in range(1, count) if counts[i] < bound]
        whole, left = sum([loads[i] for i in movable]), surplus
        for i in movable:
            extra = min(bound - counts[i], max(1, left * loads[i] // whole), surplus)
            counts[i] = counts[i] + extra
            surplus = surplus - extra
    return np.array(counts)


def scatter_about(rng, dims, deviation, most, shards=(), kind=jnp.bfloat16):
    factor_of = level_of(rng, dims, shards, -0.22, 0.18) if shards else 1.0
    values = jax.random.normal(rng, dims, jnp.float32) * deviation * factor_of
    return jnp.minimum(jnp.maximum(values, -most), most).astype(kind)


def setup_inputs(seed: int = 0) -> dict:
    streams_of = jax.random.split(jax.random.key(seed), 7)
    tokens = scatter_about(streams_of[0], (TOKENS, D), 1.0, 6.0, ((0, 256),))
    routes_keys = jax.random.split(jax.random.fold_in(streams_of[1], 1), TOKENS // TOK_DEV)
    routes_turns = jax.random.permutation(jax.random.fold_in(streams_of[1], 3), TOKENS // TOK_DEV)
    routes = jax.vmap(lambda own, number: shared_out(jax.random.fold_in(streams_of[1], 2), own, number, TOK_DEV, EXPERTS, TOP, min(2 * CAP, TOK_DEV), 2))(routes_keys, routes_turns).reshape((TOKENS, TOP))
    gates = jnp.clip(0.1 + 0.9 * jax.random.uniform(streams_of[2], (TOKENS, TOP), jnp.float32) ** level_of(streams_of[2], (TOKENS, TOP), ((0, 256),), -0.2, 0.2), 0.1, 1.0)
    cotangent = scatter_about(streams_of[3], (TOKENS, D), 1.0, 6.0, ((0, 256),))
    w_up = scatter_about(streams_of[4], (EXPERTS, D, F), D ** -0.5, 0.125, ((0, 32),))
    w_down = scatter_about(streams_of[5], (EXPERTS, F, D), F ** -0.5, 0.5, ((0, 32),))
    return dict(tokens=tokens, routes=routes, gates=gates, cotangent=cotangent, w_up=w_up, w_down=w_down)


gelu_coef = 0.7978845608028654
cubic_coef = 0.044715


def tanh_gelu(pre_act):
    inner_arg = gelu_coef * (pre_act + cubic_coef * pre_act * pre_act * pre_act)
    return 0.5 * pre_act * (1.0 + jnp.tanh(inner_arg))


def tanh_gelu_slope(pre_act):
    inner_arg = gelu_coef * (pre_act + cubic_coef * pre_act * pre_act * pre_act)
    tanh_part = jnp.tanh(inner_arg)
    return 0.5 * (1.0 + tanh_part) + 0.5 * pre_act * (1.0 - tanh_part * tanh_part) * gelu_coef * (1.0 + 3.0 * cubic_coef * pre_act * pre_act)


def route_ranks(flat_routes):
    positions = jnp.arange(flat_routes.shape[0], dtype=jnp.int32)
    matches = (flat_routes[None, :] == flat_routes[:, None]) & (positions[None, :] < positions[:, None])
    return jnp.sum(matches.astype(jnp.int32), axis=1)


def slot_table(flat_routes, experts_all, capacity):
    route_total = flat_routes.shape[0]
    ranking = route_ranks(flat_routes)
    kept_mask = ranking < capacity
    slot_index = jnp.where(kept_mask, flat_routes * capacity + ranking, experts_all * capacity).astype(jnp.int32)
    slot_route = jnp.full((experts_all * capacity + 1,), -1, jnp.int32)
    slot_route = slot_route.at[slot_index].set(jnp.arange(route_total, dtype=jnp.int32))
    return slot_route[:-1], kept_mask, slot_index


def reference(tokens, routes, gates, cotangent, w_up, w_down):
    block_total = N_EXPERT * N_DP
    route_block = TOK_DEV * TOP
    block_routes = routes.reshape(block_total, route_block)

    def per_block(one_block):
        slot_route, kept_mask, slot_index = slot_table(one_block, EXPERTS, CAP)
        return slot_route

    slot_route = lax.map(per_block, block_routes)
    block_base = (jnp.arange(block_total, dtype=jnp.int32) * route_block)[:, None]
    global_route = jnp.where(slot_route >= 0, slot_route + block_base, -1).astype(jnp.int32)
    per_expert = global_route.reshape(block_total, EXPERTS, CAP).transpose(1, 0, 2).reshape(EXPERTS, block_total * CAP)
    flat_gates = gates.reshape(-1)

    def expert_step(carry, inputs):
        mixed_acc, grad_acc = carry
        route_ids, up_mat, down_mat = inputs
        slot_valid = route_ids >= 0
        safe_route = jnp.where(slot_valid, route_ids, 0)
        token_ids = safe_route // TOP
        rows_in = jnp.where(slot_valid[:, None], tokens[token_ids], jnp.zeros((), jnp.bfloat16))
        gate_vals = jnp.where(slot_valid, flat_gates[safe_route], jnp.float32(0.0))
        slot_grads = (gate_vals[:, None] * cotangent[token_ids].astype(jnp.float32)).astype(jnp.bfloat16)
        pre_act = jnp.dot(rows_in, up_mat, preferred_element_type=jnp.float32)
        hidden = tanh_gelu(pre_act).astype(jnp.bfloat16)
        expert_out = jnp.dot(hidden, down_mat, preferred_element_type=jnp.float32).astype(jnp.bfloat16)
        mixed_acc = mixed_acc.at[token_ids].add(gate_vals[:, None] * expert_out.astype(jnp.float32))
        grad_hidden = jnp.dot(slot_grads, down_mat.T, preferred_element_type=jnp.float32)
        grad_pre = (grad_hidden * tanh_gelu_slope(pre_act)).astype(jnp.bfloat16)
        grad_rows = jnp.dot(grad_pre, up_mat.T, preferred_element_type=jnp.float32).astype(jnp.bfloat16)
        grad_acc = grad_acc.at[token_ids].add(grad_rows.astype(jnp.float32))
        rows_split = rows_in.reshape(N_EXPERT, N_DP, CAP, D).astype(jnp.float32)
        pre_split = grad_pre.reshape(N_EXPERT, N_DP, CAP, F).astype(jnp.float32)
        hidden_split = hidden.reshape(N_EXPERT, N_DP, CAP, F).astype(jnp.float32)
        grads_split = slot_grads.reshape(N_EXPERT, N_DP, CAP, D).astype(jnp.float32)
        part_up = jnp.einsum("apcd,apcf->pdf", rows_split, pre_split)
        part_down = jnp.einsum("apcf,apcd->pfd", hidden_split, grads_split)
        part_up = lax.optimization_barrier(part_up.astype(jnp.bfloat16))
        part_down = lax.optimization_barrier(part_down.astype(jnp.bfloat16))
        up_total = jnp.sum(part_up.astype(jnp.float32), axis=0).astype(jnp.bfloat16)
        down_total = jnp.sum(part_down.astype(jnp.float32), axis=0).astype(jnp.bfloat16)
        return (mixed_acc, grad_acc), (up_total, down_total)

    start_mixed = jnp.zeros((TOKENS, D), jnp.float32)
    start_grad = jnp.zeros((TOKENS, D), jnp.float32)
    carried, stacked = lax.scan(expert_step, (start_mixed, start_grad), (per_expert, w_up, w_down))
    mixed_acc, grad_acc = carried
    grad_up, grad_down = stacked
    mixed = (tokens.astype(jnp.float32) + mixed_acc).astype(jnp.bfloat16)
    token_grad = (cotangent.astype(jnp.float32) + grad_acc).astype(jnp.bfloat16)
    return mixed, token_grad, grad_up, grad_down
```

```python
import functools

import jax
import jax.numpy as jnp
from jax import lax
from jax.experimental import pallas as pl
from jax.experimental.pallas import tpu as pltpu
from jax.sharding import Mesh, PartitionSpec as P

BF = jnp.bfloat16
F32 = jnp.float32
COEF = 0.7978845608028654
CUBIC = 0.044715
NZ, NX, NY, NC = 8, 4, 4, 2
TOK, TOP, CAP, D, F = 128, 8, 4, 2048, 128
EPD = 8
EZ = EPD * NX
DS = D // NY
HS = DS // NC
SL = EZ * NY * CAP
ROWS = NZ * NY * CAP
TAB = 32
VM = pltpu.VMEM
SM = pltpu.SMEM


def params():
    return pltpu.CompilerParams(vmem_limit_bytes=56 * 1024 * 1024)


def mm(a, b, ca=1, cb=0):
    return lax.dot_general(a, b, (((ca,), (cb,)), ((), ())), preferred_element_type=F32)


def spec(*kinds):
    return [pl.BlockSpec(memory_space=k) for k in kinds]


def pack_kernel(pos, routes, gates, tokens, send):
    y = pos[2]
    lane = lax.broadcasted_iota(jnp.int32, (1, SL), 1)
    expert_of, block_of, rank_of = lane // 16, (lane // 4) % 4, lane % 4
    row = lax.broadcasted_iota(jnp.int32, (TOK, TOK), 0)
    col = lax.broadcasted_iota(jnp.int32, (TOK, TOK), 1)
    before = jnp.where(col < row, 1.0, 0.0).astype(BF)
    token = lax.broadcasted_iota(jnp.int32, (TOK, SL), 0).astype(F32) + 1.0
    tids, his, los = [], [], []
    for z in range(NZ):
        named = jnp.zeros((TOK, SL), F32)
        weight = jnp.zeros((TOK, SL), F32)
        for k in range(TOP):
            same = routes[:, k : k + 1] == expert_of + z * EZ
            named = jnp.where(same, 1.0, named)
            weight = jnp.where(same, gates[:, k : k + 1], weight)
        rank = mm(before, named.astype(BF))
        chosen = (named > 0.0) & (rank == rank_of.astype(F32)) & (block_of == y)
        tids.append(jnp.sum(jnp.where(chosen, token, 0.0), axis=0, keepdims=True))
        gate = jnp.sum(jnp.where(chosen, weight, 0.0), axis=0, keepdims=True)
        high = gate.astype(BF).astype(F32)
        his.append(high)
        los.append(gate - high)
    table = jnp.concatenate(tids + his + los + [jnp.zeros((8, SL), F32)], axis=0).astype(BF)
    for j in range(NY):
        send[j, 0:TOK, :] = tokens[:, j * DS : (j + 1) * DS]
        send[j, TOK : TOK + TAB, :] = table


def gather_kernel(turned, pos, rows, targets, own, other, slots, part):
    x, c = pos[1], pos[3]
    lane = lax.broadcasted_iota(jnp.int32, (SL, NY * TOK), 1)
    for s in range(NZ):
        hot = jnp.where(targets[:, s : s + 1] == lane, 1.0, 0.0).astype(BF)
        got = mm(hot, rows[s, 0 : NY * TOK, :]).astype(BF)
        slots[:, s * 16 : (s + 1) * 16, :] = got.reshape(EZ, 16, DS)
    cb = 1 if turned else 0
    mine = pl.ds(pl.multiple_of(c * HS, HS), HS)
    theirs = pl.ds(pl.multiple_of((1 - c) * HS, HS), HS)

    def one(i, carry):
        k, le = i // EPD, i % EPD
        e = lax.rem(x - k + NX, NX) * EPD + le
        total = mm(slots[e, :, mine], own[k, le], 1, cb) + mm(slots[e, :, theirs], other[k, le], 1, cb)
        part[e] = total.astype(BF)
        return carry

    lax.fori_loop(0, EZ, one, 0)


def combine_kernel(turned, pos, h0, h1, h2, h3, targets, own, other, out, mids, outs):
    x, y, c = pos[1], pos[2], pos[3]
    for k, h in enumerate((h0, h1, h2, h3)):
        q = lax.rem(y - k + NY, NY)
        mids[pl.ds(q * EPD, EPD)] = h[...]
    cb = 1 if turned else 0
    mine = pl.ds(pl.multiple_of(c * HS, HS), HS)
    theirs = pl.ds(pl.multiple_of((1 - c) * HS, HS), HS)

    def one(i, carry):
        k, le = i // EPD, i % EPD
        e = lax.rem(x - k + NX, NX) * EPD + le
        mid = mids[e]
        outs[e, :, mine] = mm(mid, own[k, le], 1, cb).astype(BF)
        outs[e, :, theirs] = mm(mid, other[k, le], 1, cb).astype(BF)
        return carry

    lax.fori_loop(0, EZ, one, 0)
    row = lax.broadcasted_iota(jnp.int32, (NY * TOK, SL), 0)
    for s in range(NZ):
        hot = jnp.where(targets[s : s + 1, :] == row, 1.0, 0.0).astype(BF)
        out[s] = mm(hot, outs[:, s * 16 : (s + 1) * 16, :].reshape(SL, DS)).astype(BF)


def up_kernel(pos, h0, h1, h2, h3, slots, out, mids):
    y = pos[2]
    for k, h in enumerate((h0, h1, h2, h3)):
        q = lax.rem(y - k + NY, NY)
        mids[pl.ds(q * EPD, EPD)] = h[...]

    def one(e, carry):
        grad = mm(slots[e], mids[e], 0, 0).astype(BF)
        q, le = e // EPD, e % EPD
        for half in range(NC):
            out[q, half, le] = grad[half * HS : (half + 1) * HS]
        return carry

    lax.fori_loop(0, EZ, one, 0)


def down_kernel(pos, h0, h1, h2, h3, slots, out, mids):
    y = pos[2]
    for k, h in enumerate((h0, h1, h2, h3)):
        q = lax.rem(y - k + NY, NY)
        mids[pl.ds(q * EPD, EPD)] = h[...]

    def one(e, carry):
        grad = mm(mids[e], slots[e], 0, 0).astype(BF)
        q, le = e // EPD, e % EPD
        for half in range(NC):
            out[q, half, le] = grad[:, half * HS : (half + 1) * HS]
        return carry

    lax.fori_loop(0, EZ, one, 0)


def shape(*dims):
    return jax.ShapeDtypeStruct(dims, BF)


def gather(turned, pos, rows, targets, own, other):
    return pl.pallas_call(
        functools.partial(gather_kernel, turned),
        out_shape=(shape(EZ, ROWS, DS), shape(EZ, ROWS, F)),
        in_specs=spec(SM, VM, VM, VM, VM),
        out_specs=tuple(spec(VM, VM)),
        compiler_params=params(),
        cost_estimate=pl.CostEstimate(flops=5_000_000_000, bytes_accessed=14_000_000, transcendentals=0),
    )(pos, rows, targets, own, other)


def combine(turned, pos, mids, targets, own, other):
    return pl.pallas_call(
        functools.partial(combine_kernel, turned),
        out_shape=shape(NZ, NY * TOK, DS),
        in_specs=spec(SM, VM, VM, VM, VM, VM, VM, VM),
        out_specs=spec(VM)[0],
        scratch_shapes=[VM((EZ, ROWS, F), BF), VM((EZ, ROWS, DS), BF)],
        compiler_params=params(),
        cost_estimate=pl.CostEstimate(flops=5_000_000_000, bytes_accessed=10_000_000, transcendentals=0),
    )(pos, *mids, targets, own, other)


def weight_grad(kernel, pos, mids, slots, tail):
    return pl.pallas_call(
        kernel,
        out_shape=shape(NX, NC, EPD, *tail),
        in_specs=spec(SM, VM, VM, VM, VM, VM),
        out_specs=spec(VM)[0],
        scratch_shapes=[VM((EZ, ROWS, F), BF)],
        compiler_params=params(),
        cost_estimate=pl.CostEstimate(flops=3_000_000_000, bytes_accessed=10_000_000, transcendentals=0),
    )(pos, *mids, slots)


def shift(array, axis, size, by):
    return lax.ppermute(array, axis, [(i, (i + by) % size) for i in range(size)])


def everywhere(array, axis, size):
    return [array] + [shift(array, axis, size, k) for k in range(1, size)]


def spread_weights(piece):
    own = jnp.stack(everywhere(piece, "x", NX))
    return own, shift(own, "c", NC, 1)


def exchange(array):
    return lax.all_to_all(array, "y", split_axis=0, concat_axis=0, tiled=True)


def per_device(tokens, routes, gates, cotangent, w_up, w_down):
    z, x, y, c = (lax.axis_index(name) for name in ("z", "x", "y", "c"))
    pos = jnp.stack([z, x, y, c]).astype(jnp.int32)
    send = pl.pallas_call(
        pack_kernel,
        out_shape=shape(NY, TOK + TAB, DS),
        in_specs=spec(SM, VM, VM, VM),
        out_specs=spec(VM)[0],
        compiler_params=params(),
    )(pos, routes, gates, tokens)
    relaid = exchange(send)
    table = jnp.sum(relaid[:, TOK:].astype(F32), axis=0).astype(BF)
    rows = jnp.concatenate([relaid[:, :TOK].reshape(NY * TOK, DS), table], axis=0)
    rows = lax.all_gather(rows, "z", tiled=False)
    grads_in = exchange(cotangent.reshape(TOK, NY, DS).transpose(1, 0, 2))
    grads_in = lax.all_gather(grads_in.reshape(NY * TOK, DS), "z", tiled=False)

    at = y * NC + c
    up_piece = lax.dynamic_slice_in_dim(w_up, at * HS, HS, 1)
    down_piece = lax.dynamic_slice_in_dim(w_down, at * HS, HS, 2)
    up = spread_weights(up_piece)
    down = spread_weights(down_piece)

    tables = lax.dynamic_index_in_dim(
        rows[:, NY * TOK : NY * TOK + 24].reshape(NZ, 3, NZ, SL), z, 2, keepdims=False
    ).astype(F32)
    block_of = (jnp.arange(SL, dtype=jnp.int32) // CAP) % NY
    token_of = tables[:, 0].astype(jnp.int32)
    targets = jnp.where(token_of > 0, token_of - 1 + block_of * TOK, -1)
    targets_t = targets.T
    gate_of = lax.dynamic_slice_in_dim(tables[:, 1] + tables[:, 2], y * 128, 128, 1)
    gate_of = gate_of.reshape(NZ, EPD, 16).transpose(1, 0, 2).reshape(EPD, ROWS, 1)

    slots, part = gather(False, pos, rows, targets_t, *up)
    pre = jnp.sum(exchange(part).reshape(NY, EPD, ROWS, F).astype(F32), axis=0)
    inner = jnp.tanh(COEF * (pre + CUBIC * pre * pre * pre))
    slope = 0.5 * (1.0 + inner) + 0.5 * pre * (1.0 - inner * inner) * COEF * (1.0 + 3.0 * CUBIC * pre * pre)
    hidden = (gate_of * (0.5 * pre * (1.0 + inner))).astype(BF)
    slope = gate_of * slope
    hidden = everywhere(hidden, "y", NY)
    mixed = combine(False, pos, hidden, targets, *down)
    mixed = lax.psum_scatter(mixed, "z", scatter_dimension=0, tiled=False)

    grad_slots, part = gather(True, pos, grads_in, targets_t, *down)
    down_grad = weight_grad(down_kernel, pos, hidden, grad_slots, (F, HS))
    down_grad = lax.psum_scatter(down_grad.reshape(NX * NC, EPD, F, HS), ("x", "c"), scatter_dimension=0, tiled=False)
    grad_hidden = jnp.sum(exchange(part).reshape(NY, EPD, ROWS, F).astype(F32), axis=0)
    grad_pre = everywhere((grad_hidden * slope).astype(BF), "y", NY)
    token_grad = combine(True, pos, grad_pre, targets, *up)
    token_grad = lax.psum_scatter(token_grad, "z", scatter_dimension=0, tiled=False)
    up_grad = weight_grad(up_kernel, pos, grad_pre, slots, (HS, F))
    up_grad = lax.psum_scatter(up_grad.reshape(NX * NC, EPD, HS, F), ("x", "c"), scatter_dimension=0, tiled=False)

    def finish(total, start):
        total = exchange(total.reshape(NY, TOK, DS)).transpose(1, 0, 2).reshape(TOK, D)
        return (start.astype(F32) + total.astype(F32)).astype(BF)

    return finish(mixed, tokens), finish(token_grad, cotangent), up_grad, down_grad


def solution(mesh):
    inner = Mesh(mesh.devices.reshape(NZ, NX, NY, NC), ("z", "x", "y", "c"))
    rows = P(("z", "x", "y", "c"), None)
    experts = P(("z", "x"), None, None)
    return jax.shard_map(
        per_device,
        mesh=inner,
        in_specs=(rows, rows, rows, rows, experts, experts),
        out_specs=(rows, rows, P(("z", "x"), ("y", "c"), None), P(("z", "x"), None, ("y", "c"))),
        check_vma=False,
    )
```

```python
import functools

import jax
import jax.numpy as jnp
from jax import lax
from jax.experimental import pallas as pl
from jax.experimental.pallas import tpu as pltpu
from jax.sharding import Mesh, PartitionSpec as P

BF = jnp.bfloat16
F32 = jnp.float32
COEF = 0.7978845608028654
CUBIC = 0.044715
NZ, NX, NY, NC = 8, 4, 4, 2
TOK, TOP, CAP, D, F = 128, 8, 4, 2048, 128
EPD = 8
EZ = EPD * NX
DS = D // NY
HS = DS // NC
ZT = NY * TOK
SL = EZ * NY * CAP
ROWS = NZ * NY * CAP
TAB = 32
HALF = (ZT + TAB) // 2
VM = pltpu.VMEM
SM = pltpu.SMEM


def mm(a, b, ca=1, cb=0):
    return lax.dot_general(a, b, (((ca,), (cb,)), ((), ())), preferred_element_type=F32)


def call(body, pos, inputs, outs, scratch=(), flops=0):
    single = not isinstance(outs, (list, tuple))
    shapes = [outs] if single else list(outs)
    moved = sum(a.size * a.dtype.itemsize for a in list(inputs) + shapes)
    result = pl.pallas_call(
        body,
        out_shape=tuple(shapes),
        in_specs=[pl.BlockSpec(memory_space=SM)] + [pl.BlockSpec(memory_space=VM)] * len(inputs),
        out_specs=tuple(pl.BlockSpec(memory_space=VM) for _ in shapes),
        scratch_shapes=list(scratch),
        compiler_params=pltpu.CompilerParams(vmem_limit_bytes=56 * 1024 * 1024),
        cost_estimate=pl.CostEstimate(flops=flops, bytes_accessed=moved, transcendentals=0),
    )(pos, *inputs)
    return result[0] if single else result


def bf(*dims):
    return jax.ShapeDtypeStruct(dims, BF)


def f32(*dims):
    return jax.ShapeDtypeStruct(dims, F32)


def block(index, size):
    return pl.ds(pl.multiple_of(index * size, size), size)


def pack_kernel(pos, routes, gates, tokens, cotangent, *sends):
    y = pos[2]
    lanes = EZ * CAP
    lane = lax.broadcasted_iota(jnp.int32, (1, lanes), 1)
    expert_of = (lane // CAP).astype(F32)
    rank_of = (lane % CAP).astype(F32)
    row = lax.broadcasted_iota(jnp.int32, (TOK, TOK), 0)
    col = lax.broadcasted_iota(jnp.int32, (TOK, TOK), 1)
    before = jnp.where(col < row, 1.0, 0.0).astype(BF)
    token = lax.broadcasted_iota(jnp.int32, (TOK, lanes), 0).astype(F32) + 1.0
    chosen_expert = routes[...].astype(F32).T
    weight_of = gates[...].T
    tids, his, los = [], [], []
    for z in range(NZ):
        named = jnp.zeros((TOK, lanes), F32)
        weight = jnp.zeros((TOK, lanes), F32)
        for k in range(TOP):
            same = chosen_expert[:, k : k + 1] == expert_of + float(z * EZ)
            named = jnp.where(same, 1.0, named)
            weight = jnp.where(same, weight_of[:, k : k + 1], weight)
        rank = mm(before, named.astype(BF))
        kept = (named > 0.0) & (rank == rank_of)
        tids.append(jnp.sum(jnp.where(kept, token, 0.0), axis=0, keepdims=True))
        gate = jnp.sum(jnp.where(kept, weight, 0.0), axis=0, keepdims=True)
        high = gate.astype(BF).astype(F32)
        his.append(high)
        los.append(gate - high)
    table = jnp.concatenate(tids + his + los + [jnp.zeros((8, lanes), F32)], axis=0).astype(BF)
    for k in range(NY):
        part = block(lax.rem(y + k, NY), DS)
        sends[k][0:TOK, :] = tokens[:, part]
        sends[k][TOK : TOK + TAB, :] = jnp.concatenate([table, jnp.zeros((TAB, DS - lanes), BF)], axis=1)
        sends[NY + k][...] = cotangent[:, part]


def merge_kernel(pos, r0, r1, r2, r3, out):
    y = pos[2]
    lanes = EZ * CAP
    near = lax.broadcasted_iota(jnp.int32, (lanes, SL), 0)
    far = lax.broadcasted_iota(jnp.int32, (lanes, SL), 1)
    table = jnp.zeros((TAB, SL), F32)
    for k, r in enumerate((r0, r1, r2, r3)):
        q = lax.rem(y - k + NY, NY)
        out[block(q, TOK), :] = r[0:TOK, :]
        spread = jnp.where(far == (near // CAP) * (NY * CAP) + q * CAP + near % CAP, 1.0, 0.0).astype(BF)
        table = table + mm(r[TOK : TOK + TAB, 0:lanes], spread)
    out[ZT : ZT + TAB, :] = table.astype(BF)


def merge_plain_kernel(pos, r0, r1, r2, r3, out):
    y = pos[2]
    for k, r in enumerate((r0, r1, r2, r3)):
        out[block(lax.rem(y - k + NY, NY), TOK), :] = r[...]


def first_layer(turned, pos, slots, own, other, parts):
    x, y, c = pos[1], pos[2], pos[3]
    cb = 1 if turned else 0
    mine, theirs = block(c, HS), block(1 - c, HS)
    for k in range(NY):
        q = lax.rem(y + k, NY)
        kx = lax.rem(x - q + NX, NX)
        for le in range(EPD):
            e = q * EPD + le
            total = mm(slots[e, :, mine], own[kx, le], 1, cb) + mm(slots[e, :, theirs], other[kx, le], 1, cb)
            parts[k][le] = total.astype(BF)


def token_kernel(pos, a0, u1, d1, u2, d2, u3, d3, u4, d4, own, other, slots, p0, p1, p2, p3, gate, targets, hots, far):
    z, y = pos[0], pos[2]
    far[0:HALF, :] = u4[...]
    far[HALF : 2 * HALF, :] = d4[...]
    kind = lax.broadcasted_iota(jnp.int32, (TAB, 128), 0)
    pick_token = jnp.where(kind == z, 1.0, 0.0).astype(BF)
    pick_gate = jnp.where((kind == z + 8) | (kind == z + 16), 1.0, 0.0).astype(BF)
    slot = lax.broadcasted_iota(jnp.int32, (SL, 128), 0)
    base = ((slot // CAP) % NY * TOK - 1).astype(F32)
    lane = lax.broadcasted_iota(jnp.int32, (SL, 128), 1).astype(F32)
    slot_lane = lax.broadcasted_iota(jnp.int32, (1, SL), 1)
    base_lane = ((slot_lane // CAP) % NY * TOK - 1).astype(F32)
    plane = lax.broadcasted_iota(jnp.int32, (TAB, SL), 0)
    for s, rows in enumerate((a0, u1, d1, u2, d2, u3, d3, far)):
        table = rows[ZT : ZT + TAB, :]
        token = mm(table, pick_token, 0, 0)
        target = jnp.where(token > 0.0, token + base, -1.0)
        hot = jnp.concatenate(
            [jnp.where(target == lane + float(128 * j), 1.0, 0.0).astype(BF) for j in range(NY)], axis=1
        )
        hots[s] = hot
        got = mm(hot, rows[0:ZT, :]).astype(BF)
        slots[:, s * 16 : (s + 1) * 16, :] = got.reshape(EZ, 16, DS)
        token_row = jnp.sum(jnp.where(plane == z, table.astype(F32), 0.0), axis=0, keepdims=True)
        targets[s : s + 1, :] = jnp.where(token_row > 0.0, token_row + base_lane, -1.0)
        weight = mm(rows[ZT : ZT + TAB, block(y, 128)], pick_gate, 0, 0)
        gate[:, s * 16 : (s + 1) * 16, :] = weight.reshape(EPD, 16, 128)
    first_layer(False, pos, slots, own, other, (p0, p1, p2, p3))


def cotangent_kernel(pos, a0, u1, d1, u2, d2, u3, d3, u4, d4, hots, own, other, slots, p0, p1, p2, p3, far):
    far[0 : ZT // 2, :] = u4[...]
    far[ZT // 2 : ZT, :] = d4[...]
    for s, rows in enumerate((a0, u1, d1, u2, d2, u3, d3, far)):
        got = mm(hots[s], rows[...]).astype(BF)
        slots[:, s * 16 : (s + 1) * 16, :] = got.reshape(EZ, 16, DS)
    first_layer(True, pos, slots, own, other, (p0, p1, p2, p3))


def hidden_kernel(pos, r0, r1, r2, r3, gate, hidden, slope):
    for e in range(EPD):
        pre = (r0[e].astype(F32) + r1[e].astype(F32)) + (r2[e].astype(F32) + r3[e].astype(F32))
        square = pre * pre
        inner = jnp.tanh(COEF * (pre + CUBIC * square * pre))
        weight = gate[e]
        hidden[e] = (weight * (0.5 * pre * (1.0 + inner))).astype(BF)
        slope[e] = weight * (
            0.5 * (1.0 + inner) + 0.5 * pre * (1.0 - inner * inner) * COEF * (1.0 + 3.0 * CUBIC * square)
        )


def grad_pre_kernel(pos, r0, r1, r2, r3, slope, out):
    for e in range(EPD):
        grad = (r0[e].astype(F32) + r1[e].astype(F32)) + (r2[e].astype(F32) + r3[e].astype(F32))
        out[e] = (grad * slope[e]).astype(BF)


def combine_kernel(turned, pos, h0, h1, h2, h3, targets, own, other, o0, u1, d1, u2, d2, u3, d3, u4, d4, outs):
    x, y, c = pos[1], pos[2], pos[3]
    cb = 1 if turned else 0
    mine, theirs = block(c, HS), block(1 - c, HS)
    for k, h in enumerate((h0, h1, h2, h3)):
        q = lax.rem(y - k + NY, NY)
        kx = lax.rem(x - q + NX, NX)
        for le in range(EPD):
            e = q * EPD + le
            outs[e, :, mine] = mm(h[le], own[kx, le], 1, cb).astype(BF)
            outs[e, :, theirs] = mm(h[le], other[kx, le], 1, cb).astype(BF)
    row = lax.broadcasted_iota(jnp.int32, (ZT, SL), 0).astype(F32)
    for s, out in enumerate((o0, u1, d1, u2, d2, u3, d3, None)):
        hot = jnp.where(targets[s : s + 1, :] == row, 1.0, 0.0).astype(BF)
        total = mm(hot, outs[:, s * 16 : (s + 1) * 16, :].reshape(SL, DS)).astype(BF)
        if out is None:
            u4[...] = total[: ZT // 2]
            d4[...] = total[ZT // 2 :]
        else:
            out[...] = total


def weight_grad_kernel(up, pos, h0, h1, h2, h3, slots, keep, give):
    x, y, c = pos[1], pos[2], pos[3]
    for k, h in enumerate((h0, h1, h2, h3)):
        q = lax.rem(y - k + NY, NY)
        kx = lax.rem(q - x + NX, NX)
        for le in range(EPD):
            for out, half in ((keep, c), (give, 1 - c)):
                rows = slots[q * EPD + le, :, block(half, HS)]
                grad = mm(rows, h[le], 0, 0) if up else mm(h[le], rows, 0, 0)
                out[kx, le] = grad.astype(BF)


def split_kernel(pos, own, up, down, s0, s1, s2, s3):
    y = pos[2]
    for k, out in enumerate((s0, s1, s2, s3)):
        rows = block(lax.rem(y + k, NY), TOK)
        out[...] = (
            own[rows, :].astype(F32) + up[rows, :].astype(F32) + down[rows, :].astype(F32)
        ).astype(BF)


def finish_kernel(pos, r0, r1, r2, r3, start, out):
    y = pos[2]
    for k, r in enumerate((r0, r1, r2, r3)):
        part = block(lax.rem(y - k + NY, NY), DS)
        out[:, part] = (start[:, part].astype(F32) + r[...].astype(F32)).astype(BF)


def shift(array, axis, size, by):
    return lax.ppermute(array, axis, [(i, (i + by) % size) for i in range(size)])


def everywhere(array, axis, size):
    return [array] + [shift(array, axis, size, k) for k in range(1, size)]


def exchange(arrays, axis, size):
    return [arrays[0]] + [shift(arrays[k], axis, size, k) for k in range(1, size)]


def add(a, b):
    return (a.astype(F32) + b.astype(F32)).astype(BF)


def ring_gather(own, half):
    chunks, up, down = [own], own, own
    for _ in range(3):
        up, down = shift(up, "z", NZ, 1), shift(down, "z", NZ, -1)
        chunks += [up, down]
    return chunks + [shift(up[:half], "z", NZ, 1), shift(down[half:], "z", NZ, -1)]


def ring_sum(pos, chunks):
    half = ZT // 2
    own, u1, d1, u2, d2, u3, d3, u4, d4 = chunks
    back, on = shift(u4, "z", NZ, -1), shift(d4, "z", NZ, 1)
    back = shift(jnp.concatenate([add(u3[:half], back), u3[half:]], axis=0), "z", NZ, -1)
    on = shift(jnp.concatenate([d3[:half], add(d3[half:], on)], axis=0), "z", NZ, 1)
    back, on = shift(add(u2, back), "z", NZ, -1), shift(add(d2, on), "z", NZ, 1)
    back, on = shift(add(u1, back), "z", NZ, -1), shift(add(d1, on), "z", NZ, 1)
    pieces = call(split_kernel, pos, [own, back, on], [bf(TOK, DS)] * NY)
    return exchange(pieces, "y", NY)


def spread_weights(piece):
    own = jnp.stack(everywhere(piece, "x", NX))
    return own, shift(own, "c", NC, 1)


def weight_grad(up, pos, mids, slots):
    tail = (HS, F) if up else (F, HS)
    keep, give = call(
        functools.partial(weight_grad_kernel, up),
        pos,
        [*mids, slots],
        [bf(NX, EPD, *tail)] * 2,
        flops=2_000_000_000,
    )
    total = add(keep, shift(give, "c", NC, 1))
    got = exchange([total[k] for k in range(NX)], "x", NX)
    return functools.reduce(lambda a, b: a + b, [g.astype(F32) for g in got]).astype(BF)


def per_device(tokens, routes, gates, cotangent, w_up, w_down):
    z, x, y, c = (lax.axis_index(name) for name in ("z", "x", "y", "c"))
    pos = jnp.stack([z, x, y, c]).astype(jnp.int32)
    sends = call(
        pack_kernel,
        pos,
        [routes.T, gates.T, tokens, cotangent],
        [bf(TOK + TAB, DS)] * NY + [bf(TOK, DS)] * NY,
    )
    relaid = exchange(sends[:NY], "y", NY)
    rows = ring_gather(call(merge_kernel, pos, relaid, bf(ZT + TAB, DS)), HALF)
    relaid = exchange(sends[NY:], "y", NY)
    grads_in = ring_gather(call(merge_plain_kernel, pos, relaid, bf(ZT, DS)), ZT // 2)

    at = y * NC + c
    up = spread_weights(lax.dynamic_slice_in_dim(w_up, at * HS, HS, 1))
    down = spread_weights(lax.dynamic_slice_in_dim(w_down, at * HS, HS, 2))

    part = [bf(EPD, ROWS, F)] * NY
    slots, p0, p1, p2, p3, gate, targets, hots = call(
        token_kernel,
        pos,
        [*rows, *up],
        [bf(EZ, ROWS, DS), *part, f32(EPD, ROWS, F), f32(NZ, SL), bf(NZ, SL, ZT)],
        [VM((ZT + TAB, DS), BF)],
        flops=5_000_000_000,
    )
    pre = exchange([p0, p1, p2, p3], "y", NY)
    hidden, slope = call(hidden_kernel, pos, [*pre, gate], [bf(EPD, ROWS, F), f32(EPD, ROWS, F)], flops=10_000_000)
    hidden = everywhere(hidden, "y", NY)
    outs = [bf(ZT, DS)] * 7 + [bf(ZT // 2, DS)] * 2
    work = [VM((EZ, ROWS, DS), BF)]
    mixed = call(
        functools.partial(combine_kernel, False), pos, [*hidden, targets, *down], outs, work, flops=5_000_000_000
    )
    mixed = ring_sum(pos, mixed)

    grad_slots, p0, p1, p2, p3 = call(
        cotangent_kernel,
        pos,
        [*grads_in, hots, *down],
        [bf(EZ, ROWS, DS), *part],
        [VM((ZT, DS), BF)],
        flops=5_000_000_000,
    )
    grads = exchange([p0, p1, p2, p3], "y", NY)
    grad_pre = everywhere(call(grad_pre_kernel, pos, [*grads, slope], bf(EPD, ROWS, F)), "y", NY)
    token_grad = call(
        functools.partial(combine_kernel, True), pos, [*grad_pre, targets, *up], outs, work, flops=5_000_000_000
    )
    token_grad = ring_sum(pos, token_grad)
    down_grad = weight_grad(False, pos, hidden, grad_slots)
    up_grad = weight_grad(True, pos, grad_pre, slots)
    mixed = call(finish_kernel, pos, [*mixed, tokens], bf(TOK, D))
    token_grad = call(finish_kernel, pos, [*token_grad, cotangent], bf(TOK, D))
    return mixed, token_grad, up_grad, down_grad


def solution(mesh):
    inner = Mesh(mesh.devices.reshape(NZ, NX, NY, NC), ("z", "x", "y", "c"))
    rows = P(("z", "x", "y", "c"), None)
    experts = P(("z", "x"), None, None)
    return jax.shard_map(
        per_device,
        mesh=inner,
        in_specs=(rows, rows, rows, rows, experts, experts),
        out_specs=(rows, rows, P(("z", "x"), ("y", "c"), None), P(("z", "x"), None, ("y", "c"))),
        check_vma=False,
    )
```

```python
import functools

import jax
import jax.numpy as jnp
from jax import lax
from jax.experimental import pallas as pl
from jax.experimental.pallas import tpu as pltpu
from jax.sharding import Mesh, PartitionSpec as P

BF = jnp.bfloat16
F32 = jnp.float32
COEF = 0.7978845608028654
CUBIC = 0.044715
NZ, NX, NY, NC = 8, 4, 4, 2
TOK, TOP, CAP, D, F = 128, 8, 4, 2048, 128
EPD = 8
EZ = EPD * NX
DS = D // NY
HS = DS // NC
ZT = NY * TOK
SL = EZ * NY * CAP
ROWS = NZ * NY * CAP
TAB = 32
VM = pltpu.VMEM
SM = pltpu.SMEM


def mm(a, b, ca=1, cb=0):
    return lax.dot_general(a, b, (((ca,), (cb,)), ((), ())), preferred_element_type=F32)


def call(body, pos, inputs, outs, scratch=(), flops=2_300_000_000):
    single = not isinstance(outs, (list, tuple))
    shapes = [outs] if single else list(outs)
    moved = sum(a.size * a.dtype.itemsize for a in list(inputs) + shapes)
    result = pl.pallas_call(
        body,
        out_shape=tuple(shapes),
        in_specs=[pl.BlockSpec(memory_space=SM)] + [pl.BlockSpec(memory_space=VM)] * len(inputs),
        out_specs=tuple(pl.BlockSpec(memory_space=VM) for _ in shapes),
        scratch_shapes=list(scratch),
        compiler_params=pltpu.CompilerParams(vmem_limit_bytes=56 * 1024 * 1024),
        cost_estimate=pl.CostEstimate(flops=flops, bytes_accessed=moved, transcendentals=0),
    )(pos, *inputs)
    return result[0] if single else result


def bf(*dims):
    return jax.ShapeDtypeStruct(dims, BF)


def f32(*dims):
    return jax.ShapeDtypeStruct(dims, F32)


def block(index, size):
    return pl.ds(pl.multiple_of(index * size, size), size)


def pack_kernel(pos, routes, gates, tokens, cotangent, *sends):
    y = pos[2]
    lanes = EZ * CAP
    lane = lax.broadcasted_iota(jnp.int32, (1, lanes), 1)
    expert_of = (lane // CAP).astype(F32)
    rank_of = (lane % CAP).astype(F32)
    row = lax.broadcasted_iota(jnp.int32, (TOK, TOK), 0)
    col = lax.broadcasted_iota(jnp.int32, (TOK, TOK), 1)
    before = jnp.where(col < row, 1.0, 0.0).astype(BF)
    token = lax.broadcasted_iota(jnp.int32, (TOK, lanes), 0).astype(F32) + 1.0
    chosen_expert = routes[...].astype(F32).T
    weight_of = gates[...].T
    tids, his, los = [], [], []
    for z in range(NZ):
        named = jnp.zeros((TOK, lanes), F32)
        weight = jnp.zeros((TOK, lanes), F32)
        for k in range(TOP):
            same = chosen_expert[:, k : k + 1] == expert_of + float(z * EZ)
            named = jnp.where(same, 1.0, named)
            weight = jnp.where(same, weight_of[:, k : k + 1], weight)
        rank = mm(before, named.astype(BF))
        kept = (named > 0.0) & (rank == rank_of)
        tids.append(jnp.sum(jnp.where(kept, token, 0.0), axis=0, keepdims=True))
        gate = jnp.sum(jnp.where(kept, weight, 0.0), axis=0, keepdims=True)
        high = gate.astype(BF).astype(F32)
        his.append(high)
        los.append(gate - high)
    table = jnp.concatenate(tids + his + los + [jnp.zeros((8, lanes), F32)], axis=0).astype(BF)
    for k in range(NY):
        part = block(lax.rem(y + k, NY), DS)
        sends[k][0:TOK, :] = tokens[:, part]
        sends[k][TOK : TOK + TAB, :] = jnp.concatenate([table, jnp.zeros((TAB, DS - lanes), BF)], axis=1)
        sends[NY + k][...] = cotangent[:, part]


def merge_kernel(pos, r0, r1, r2, r3, out):
    y = pos[2]
    lanes = EZ * CAP
    near = lax.broadcasted_iota(jnp.int32, (lanes, SL), 0)
    far = lax.broadcasted_iota(jnp.int32, (lanes, SL), 1)
    table = jnp.zeros((TAB, SL), F32)
    for k, r in enumerate((r0, r1, r2, r3)):
        q = lax.rem(y - k + NY, NY)
        out[block(q, TOK), :] = r[0:TOK, :]
        spread = jnp.where(far == (near // CAP) * (NY * CAP) + q * CAP + near % CAP, 1.0, 0.0).astype(BF)
        table = table + mm(r[TOK : TOK + TAB, 0:lanes], spread)
    out[ZT : ZT + TAB, :] = table.astype(BF)


def merge_plain_kernel(pos, r0, r1, r2, r3, out):
    y = pos[2]
    for k, r in enumerate((r0, r1, r2, r3)):
        out[block(lax.rem(y - k + NY, NY), TOK), :] = r[...]


def first_layer(turned, pos, slots, own, other, parts):
    x, y, c = pos[1], pos[2], pos[3]
    cb = 1 if turned else 0
    mine, theirs = block(c, HS), block(1 - c, HS)
    for k in range(NY):
        q = lax.rem(y + k, NY)
        kx = lax.rem(x - q + NX, NX)
        for le in range(EPD):
            e = q * EPD + le
            total = mm(slots[e, :, mine], own[kx, le], 1, cb) + mm(slots[e, :, theirs], other[kx, le], 1, cb)
            parts[k][le] = total.astype(BF)


def token_kernel(pos, sources, own, other, slots, p0, p1, p2, p3, gate, targets, hots):
    z, y = pos[0], pos[2]
    kind = lax.broadcasted_iota(jnp.int32, (TAB, 128), 0)
    pick_token = jnp.where(kind == z, 1.0, 0.0).astype(BF)
    pick_gate = jnp.where((kind == z + 8) | (kind == z + 16), 1.0, 0.0).astype(BF)
    slot = lax.broadcasted_iota(jnp.int32, (SL, 128), 0)
    base = ((slot // CAP) % NY * TOK - 1).astype(F32)
    lane = lax.broadcasted_iota(jnp.int32, (SL, 128), 1).astype(F32)
    slot_lane = lax.broadcasted_iota(jnp.int32, (1, SL), 1)
    base_lane = ((slot_lane // CAP) % NY * TOK - 1).astype(F32)
    plane = lax.broadcasted_iota(jnp.int32, (TAB, SL), 0)
    for s in range(NZ):
        rows = sources.at[s]
        table = rows[ZT : ZT + TAB, :]
        token = mm(table, pick_token, 0, 0)
        target = jnp.where(token > 0.0, token + base, -1.0)
        hot = jnp.concatenate(
            [jnp.where(target == lane + float(128 * j), 1.0, 0.0).astype(BF) for j in range(NY)], axis=1
        )
        hots[s] = hot
        got = mm(hot, rows[0:ZT, :]).astype(BF)
        slots[:, s * 16 : (s + 1) * 16, :] = got.reshape(EZ, 16, DS)
        token_row = jnp.sum(jnp.where(plane == z, table.astype(F32), 0.0), axis=0, keepdims=True)
        targets[s : s + 1, :] = jnp.where(token_row > 0.0, token_row + base_lane, -1.0)
        weight = mm(rows[ZT : ZT + TAB, block(y, 128)], pick_gate, 0, 0)
        gate[:, s * 16 : (s + 1) * 16, :] = weight.reshape(EPD, 16, 128)
    first_layer(False, pos, slots, own, other, (p0, p1, p2, p3))


def cotangent_kernel(pos, sources, hots, own, other, slots, p0, p1, p2, p3):
    for s in range(NZ):
        got = mm(hots[s], sources[s]).astype(BF)
        slots[:, s * 16 : (s + 1) * 16, :] = got.reshape(EZ, 16, DS)
    first_layer(True, pos, slots, own, other, (p0, p1, p2, p3))


def hidden_kernel(pos, r0, r1, r2, r3, gate, hidden, slope):
    for e in range(EPD):
        pre = (r0[e].astype(F32) + r1[e].astype(F32)) + (r2[e].astype(F32) + r3[e].astype(F32))
        square = pre * pre
        inner = jnp.tanh(COEF * (pre + CUBIC * square * pre))
        weight = gate[e]
        hidden[e] = (weight * (0.5 * pre * (1.0 + inner))).astype(BF)
        slope[e] = weight * (
            0.5 * (1.0 + inner) + 0.5 * pre * (1.0 - inner * inner) * COEF * (1.0 + 3.0 * CUBIC * square)
        )


def grad_pre_kernel(pos, r0, r1, r2, r3, slope, out):
    for e in range(EPD):
        grad = (r0[e].astype(F32) + r1[e].astype(F32)) + (r2[e].astype(F32) + r3[e].astype(F32))
        out[e] = (grad * slope[e]).astype(BF)


def combine_kernel(turned, pos, h0, h1, h2, h3, targets, own, other, out, outs):
    x, y, c = pos[1], pos[2], pos[3]
    cb = 1 if turned else 0
    mine, theirs = block(c, HS), block(1 - c, HS)
    for k, h in enumerate((h0, h1, h2, h3)):
        q = lax.rem(y - k + NY, NY)
        kx = lax.rem(x - q + NX, NX)
        for le in range(EPD):
            e = q * EPD + le
            outs[e, :, mine] = mm(h[le], own[kx, le], 1, cb).astype(BF)
            outs[e, :, theirs] = mm(h[le], other[kx, le], 1, cb).astype(BF)
    row = lax.broadcasted_iota(jnp.int32, (ZT, SL), 0).astype(F32)
    for s in range(NZ):
        hot = jnp.where(targets[s : s + 1, :] == row, 1.0, 0.0).astype(BF)
        out[s] = mm(hot, outs[:, s * 16 : (s + 1) * 16, :].reshape(SL, DS)).astype(BF)


def weight_grad_kernel(up, pos, h0, h1, h2, h3, slots, keep, give):
    x, y, c = pos[1], pos[2], pos[3]
    for k, h in enumerate((h0, h1, h2, h3)):
        q = lax.rem(y - k + NY, NY)
        kx = lax.rem(q - x + NX, NX)
        for le in range(EPD):
            for out, half in ((keep, c), (give, 1 - c)):
                rows = slots[q * EPD + le, :, block(half, HS)]
                grad = mm(rows, h[le], 0, 0) if up else mm(h[le], rows, 0, 0)
                out[kx, le] = grad.astype(BF)


def split_kernel(pos, total, s0, s1, s2, s3):
    y = pos[2]
    for k, out in enumerate((s0, s1, s2, s3)):
        out[...] = total[block(lax.rem(y + k, NY), TOK), :]


def finish_kernel(pos, r0, r1, r2, r3, start, out):
    y = pos[2]
    for k, r in enumerate((r0, r1, r2, r3)):
        part = block(lax.rem(y - k + NY, NY), DS)
        out[:, part] = (start[:, part].astype(F32) + r[...].astype(F32)).astype(BF)


def shift(array, axis, size, by):
    return lax.ppermute(array, axis, [(i, (i + by) % size) for i in range(size)])


def everywhere(array, axis, size):
    return [array] + [shift(array, axis, size, k) for k in range(1, size)]


def exchange(arrays, axis, size):
    return [arrays[0]] + [shift(arrays[k], axis, size, k) for k in range(1, size)]


def add(a, b):
    return (a.astype(F32) + b.astype(F32)).astype(BF)


def after(value, *others):
    return lax.optimization_barrier((value, *others))[0]


def gather_z(array):
    return lax.all_gather(array, "z", tiled=False)


def sum_z(array):
    return lax.psum_scatter(array, "z", scatter_dimension=0, tiled=False)


def back_to_tokens(pos, total, start):
    pieces = exchange(call(split_kernel, pos, [total], [bf(TOK, DS)] * NY), "y", NY)
    return call(finish_kernel, pos, [*pieces, start], bf(TOK, D))


def spread_weights(piece):
    own = jnp.stack(everywhere(piece, "x", NX))
    return own, shift(own, "c", NC, 1)


def weight_grad_parts(up, pos, mids, slots):
    tail = (HS, F) if up else (F, HS)
    return call(
        functools.partial(weight_grad_kernel, up),
        pos,
        [*mids, slots],
        [bf(NX, EPD, *tail)] * 2,
        flops=7_000_000_000,
    )


def weight_grad(keep, give):
    total = add(keep, shift(give, "c", NC, 1))
    return total, exchange([total[k] for k in range(NX)], "x", NX)


def total_of(arrays):
    return functools.reduce(lambda a, b: a + b, [a.astype(F32) for a in arrays]).astype(BF)


def per_device(tokens, routes, gates, cotangent, w_up, w_down):
    z, x, y, c = (lax.axis_index(name) for name in ("z", "x", "y", "c"))
    pos = jnp.stack([z, x, y, c]).astype(jnp.int32)
    sends = call(
        pack_kernel,
        pos,
        [routes.T, gates.T, tokens, cotangent],
        [bf(TOK + TAB, DS)] * NY + [bf(TOK, DS)] * NY,
        flops=4_000_000_000,
    )
    relaid = exchange(sends[:NY], "y", NY)
    start = call(merge_kernel, pos, relaid, bf(ZT + TAB, DS))
    rows = gather_z(start)
    relaid = exchange(after(list(sends[NY:]), start), "y", NY)
    grad_start = call(merge_plain_kernel, pos, relaid, bf(ZT, DS))
    grads_in = gather_z(grad_start)

    at = y * NC + c
    up = spread_weights(after(lax.dynamic_slice_in_dim(w_up, at * HS, HS, 1), grad_start))
    down = everywhere(after(lax.dynamic_slice_in_dim(w_down, at * HS, HS, 2), grad_start), "x", NX)
    rows = after(rows, *up)

    part = [bf(EPD, ROWS, F)] * NY
    slots, p0, p1, p2, p3, gate, targets, hots = call(
        token_kernel,
        pos,
        [rows, *up],
        [bf(EZ, ROWS, DS), *part, f32(EPD, ROWS, F), f32(NZ, SL), bf(NZ, SL, ZT)],
        flops=13_000_000_000,
    )
    down = jnp.stack(after(down, p0))
    down = (down, shift(down, "c", NC, 1))
    pre = exchange([p0, p1, p2, p3], "y", NY)
    hidden, slope = call(hidden_kernel, pos, [*pre, gate], [bf(EPD, ROWS, F), f32(EPD, ROWS, F)])
    hidden = everywhere(hidden, "y", NY)
    outs = bf(NZ, ZT, DS)
    work = [VM((EZ, ROWS, DS), BF)]
    mixed = call(
        functools.partial(combine_kernel, False), pos, [*hidden, targets, *down], outs, work, flops=8_000_000_000
    )
    grad_slots, p0, p1, p2, p3 = call(
        cotangent_kernel,
        pos,
        [after(grads_in, mixed), hots, *down],
        [bf(EZ, ROWS, DS), *part],
        flops=11_000_000_000,
    )
    mixed = sum_z(mixed)
    keep, give = weight_grad_parts(False, pos, hidden, grad_slots)
    grads = after(exchange([p0, p1, p2, p3], "y", NY), keep)
    grad_pre = everywhere(call(grad_pre_kernel, pos, [*grads, slope], bf(EPD, ROWS, F)), "y", NY)
    down_total, down_parts = weight_grad(keep, give)
    grad_pre = after(grad_pre, down_total)
    token_grad = call(
        functools.partial(combine_kernel, True), pos, [*grad_pre, targets, *up], outs, work, flops=8_000_000_000
    )
    _, up_parts = weight_grad(*weight_grad_parts(True, pos, after(grad_pre, token_grad), slots))
    token_grad = sum_z(token_grad)
    mixed = back_to_tokens(pos, mixed, tokens)
    up_grad, down_grad = total_of(up_parts), total_of(down_parts)
    token_grad = back_to_tokens(pos, after(token_grad, up_grad, down_grad, mixed), cotangent)
    return mixed, token_grad, up_grad, down_grad


def solution(mesh):
    inner = Mesh(mesh.devices.reshape(NZ, NX, NY, NC), ("z", "x", "y", "c"))
    rows = P(("z", "x", "y", "c"), None)
    experts = P(("z", "x"), None, None)
    return jax.shard_map(
        per_device,
        mesh=inner,
        in_specs=(rows, rows, rows, rows, experts, experts),
        out_specs=(rows, rows, P(("z", "x"), ("y", "c"), None), P(("z", "x"), None, ("y", "c"))),
        check_vma=False,
    )
```

```python
import functools

import jax
import jax.numpy as jnp
from jax import lax
from jax.experimental import pallas as pl
from jax.experimental.pallas import tpu as pltpu
from jax.sharding import Mesh, PartitionSpec as P

BF = jnp.bfloat16
F32 = jnp.float32
COEF = 0.7978845608028654
CUBIC = 0.044715
NZ, NX, NY, NC = 8, 4, 4, 2
TOK, TOP, CAP, D, F = 128, 8, 4, 2048, 128
EPD = 8
EZ = EPD * NX
DS = D // NY
HS = DS // NC
ZT = NY * TOK
SL = EZ * NY * CAP
ROWS = NZ * NY * CAP
TAB = 16
VM = pltpu.VMEM
SM = pltpu.SMEM


def mm(a, b, ca=1, cb=0):
    return lax.dot_general(a, b, (((ca,), (cb,)), ((), ())), preferred_element_type=F32)


def call(body, pos, inputs, outs, scratch=(), flops=2_300_000_000):
    single = not isinstance(outs, (list, tuple))
    shapes = [outs] if single else list(outs)
    moved = sum(a.size * a.dtype.itemsize for a in list(inputs) + shapes)
    result = pl.pallas_call(
        body,
        out_shape=tuple(shapes),
        in_specs=[pl.BlockSpec(memory_space=SM)] + [pl.BlockSpec(memory_space=VM)] * len(inputs),
        out_specs=tuple(pl.BlockSpec(memory_space=VM) for _ in shapes),
        scratch_shapes=list(scratch),
        compiler_params=pltpu.CompilerParams(vmem_limit_bytes=56 * 1024 * 1024),
        cost_estimate=pl.CostEstimate(flops=flops, bytes_accessed=moved, transcendentals=0),
    )(pos, *inputs)
    return result[0] if single else result


def bf(*dims):
    return jax.ShapeDtypeStruct(dims, BF)


def f32(*dims):
    return jax.ShapeDtypeStruct(dims, F32)


def block(index, size):
    return pl.ds(pl.multiple_of(index * size, size), size)


def pack_kernel(pos, routes, gates, tokens, cotangent, *sends):
    y = pos[2]
    lanes = EZ * CAP
    lane = lax.broadcasted_iota(jnp.int32, (1, lanes), 1)
    expert_of = (lane // CAP).astype(F32)
    rank_of = (lane % CAP).astype(F32)
    row = lax.broadcasted_iota(jnp.int32, (TOK, TOK), 0)
    col = lax.broadcasted_iota(jnp.int32, (TOK, TOK), 1)
    before = jnp.where(col < row, 1.0, 0.0).astype(BF)
    token = lax.broadcasted_iota(jnp.int32, (TOK, lanes), 0).astype(F32) + 1.0
    chosen_expert = routes[...].astype(F32).T
    weight_of = gates[...].T
    tids, weights = [], []
    for z in range(NZ):
        named = jnp.zeros((TOK, lanes), F32)
        weight = jnp.zeros((TOK, lanes), F32)
        for k in range(TOP):
            same = chosen_expert[:, k : k + 1] == expert_of + float(z * EZ)
            named = jnp.where(same, 1.0, named)
            weight = jnp.where(same, weight_of[:, k : k + 1], weight)
        rank = mm(before, named.astype(BF))
        kept = (named > 0.0) & (rank == rank_of)
        tids.append(jnp.sum(jnp.where(kept, token, 0.0), axis=0, keepdims=True))
        weights.append(jnp.sum(jnp.where(kept, weight, 0.0), axis=0, keepdims=True))
    table = jnp.concatenate(tids + weights, axis=0).astype(BF)
    for k in range(NY):
        part = block(lax.rem(y + k, NY), DS)
        sends[k][0:TOK, :] = tokens[:, part]
        sends[k][TOK : TOK + TAB, :] = jnp.concatenate([table, jnp.zeros((TAB, DS - lanes), BF)], axis=1)
        sends[NY + k][...] = cotangent[:, part]


def merge_kernel(pos, r0, r1, r2, r3, out):
    y = pos[2]
    lanes = EZ * CAP
    near = lax.broadcasted_iota(jnp.int32, (lanes, SL), 0)
    far = lax.broadcasted_iota(jnp.int32, (lanes, SL), 1)
    table = jnp.zeros((TAB, SL), F32)
    for k, r in enumerate((r0, r1, r2, r3)):
        q = lax.rem(y - k + NY, NY)
        out[block(q, TOK), :] = r[0:TOK, :]
        spread = jnp.where(far == (near // CAP) * (NY * CAP) + q * CAP + near % CAP, 1.0, 0.0).astype(BF)
        table = table + mm(r[TOK : TOK + TAB, 0:lanes], spread)
    out[ZT : ZT + TAB, :] = table.astype(BF)


def merge_plain_kernel(pos, r0, r1, r2, r3, out):
    y = pos[2]
    for k, r in enumerate((r0, r1, r2, r3)):
        out[block(lax.rem(y - k + NY, NY), TOK), :] = r[...]


def first_layer(turned, pos, slots, own, other, parts):
    x, y, c = pos[1], pos[2], pos[3]
    cb = 1 if turned else 0
    mine, theirs = block(c, HS), block(1 - c, HS)
    for k in range(NY):
        q = lax.rem(y + k, NY)
        kx = lax.rem(x - q + NX, NX)
        for le in range(EPD):
            e = q * EPD + le
            total = mm(slots[e, :, mine], own[kx, le], 1, cb) + mm(slots[e, :, theirs], other[kx, le], 1, cb)
            parts[k][le] = total.astype(BF)


def token_kernel(pos, sources, own, other, slots, p0, p1, p2, p3, gate, targets, hots):
    z, y = pos[0], pos[2]
    kind = lax.broadcasted_iota(jnp.int32, (TAB, 128), 0)
    pick_token = jnp.where(kind == z, 1.0, 0.0).astype(BF)
    pick_gate = jnp.where(kind == z + 8, 1.0, 0.0).astype(BF)
    slot = lax.broadcasted_iota(jnp.int32, (SL, 128), 0)
    base = ((slot // CAP) % NY * TOK - 1).astype(F32)
    lane = lax.broadcasted_iota(jnp.int32, (SL, 128), 1).astype(F32)
    slot_lane = lax.broadcasted_iota(jnp.int32, (1, SL), 1)
    base_lane = ((slot_lane // CAP) % NY * TOK - 1).astype(F32)
    plane = lax.broadcasted_iota(jnp.int32, (TAB, SL), 0)
    for s in range(NZ):
        rows = sources.at[s]
        table = rows[ZT : ZT + TAB, :]
        token = mm(table, pick_token, 0, 0)
        target = jnp.where(token > 0.0, token + base, -1.0)
        hot = jnp.concatenate(
            [jnp.where(target == lane + float(128 * j), 1.0, 0.0).astype(BF) for j in range(NY)], axis=1
        )
        hots[s] = hot
        got = mm(hot, rows[0:ZT, :]).astype(BF)
        slots[:, s * 16 : (s + 1) * 16, :] = got.reshape(EZ, 16, DS)
        token_row = jnp.sum(jnp.where(plane == z, table.astype(F32), 0.0), axis=0, keepdims=True)
        targets[s : s + 1, :] = jnp.where(token_row > 0.0, token_row + base_lane, -1.0)
        weight = mm(rows[ZT : ZT + TAB, block(y, 128)], pick_gate, 0, 0)
        gate[:, s * 16 : (s + 1) * 16, :] = weight.reshape(EPD, 16, 128)
    first_layer(False, pos, slots, own, other, (p0, p1, p2, p3))


def cotangent_kernel(pos, sources, hots, own, other, slots, p0, p1, p2, p3):
    for s in range(NZ):
        got = mm(hots[s], sources[s]).astype(BF)
        slots[:, s * 16 : (s + 1) * 16, :] = got.reshape(EZ, 16, DS)
    first_layer(True, pos, slots, own, other, (p0, p1, p2, p3))


def hidden_kernel(pos, r0, r1, r2, r3, gate, hidden, slope):
    for e in range(EPD):
        pre = (r0[e].astype(F32) + r1[e].astype(F32)) + (r2[e].astype(F32) + r3[e].astype(F32))
        square = pre * pre
        inner = jnp.tanh(COEF * (pre + CUBIC * square * pre))
        weight = gate[e]
        hidden[e] = (weight * (0.5 * pre * (1.0 + inner))).astype(BF)
        slope[e] = weight * (
            0.5 * (1.0 + inner) + 0.5 * pre * (1.0 - inner * inner) * COEF * (1.0 + 3.0 * CUBIC * square)
        )


def grad_pre_kernel(pos, r0, r1, r2, r3, slope, out):
    for e in range(EPD):
        grad = (r0[e].astype(F32) + r1[e].astype(F32)) + (r2[e].astype(F32) + r3[e].astype(F32))
        out[e] = (grad * slope[e]).astype(BF)


def combine_kernel(turned, pos, h0, h1, h2, h3, targets, own, other, out, outs):
    x, y, c = pos[1], pos[2], pos[3]
    cb = 1 if turned else 0
    mine, theirs = block(c, HS), block(1 - c, HS)
    for k, h in enumerate((h0, h1, h2, h3)):
        q = lax.rem(y - k + NY, NY)
        kx = lax.rem(x - q + NX, NX)
        for le in range(EPD):
            e = q * EPD + le
            outs[e, :, mine] = mm(h[le], own[kx, le], 1, cb).astype(BF)
            outs[e, :, theirs] = mm(h[le], other[kx, le], 1, cb).astype(BF)
    row = lax.broadcasted_iota(jnp.int32, (ZT, SL), 0).astype(F32)
    for s in range(NZ):
        hot = jnp.where(targets[s : s + 1, :] == row, 1.0, 0.0).astype(BF)
        out[s] = mm(hot, outs[:, s * 16 : (s + 1) * 16, :].reshape(SL, DS)).astype(BF)


def weight_grad_kernel(up, pos, h0, h1, h2, h3, slots, keep, give):
    x, y, c = pos[1], pos[2], pos[3]
    for k, h in enumerate((h0, h1, h2, h3)):
        q = lax.rem(y - k + NY, NY)
        kx = lax.rem(q - x + NX, NX)
        for le in range(EPD):
            for out, half in ((keep, c), (give, 1 - c)):
                rows = slots[q * EPD + le, :, block(half, HS)]
                grad = mm(rows, h[le], 0, 0) if up else mm(h[le], rows, 0, 0)
                out[kx, le] = grad.astype(BF)


def split_kernel(pos, total, s0, s1, s2, s3):
    y = pos[2]
    for k, out in enumerate((s0, s1, s2, s3)):
        out[...] = total[block(lax.rem(y + k, NY), TOK), :]


def finish_kernel(pos, r0, r1, r2, r3, start, out):
    y = pos[2]
    for k, r in enumerate((r0, r1, r2, r3)):
        part = block(lax.rem(y - k + NY, NY), DS)
        out[:, part] = (start[:, part].astype(F32) + r[...].astype(F32)).astype(BF)


def shift(array, axis, size, by):
    return lax.ppermute(array, axis, [(i, (i + by) % size) for i in range(size)])


def everywhere(array, axis, size):
    return [array] + [shift(array, axis, size, k) for k in range(1, size)]


def exchange(arrays, axis, size):
    return [arrays[0]] + [shift(arrays[k], axis, size, k) for k in range(1, size)]


def add(a, b):
    return (a.astype(F32) + b.astype(F32)).astype(BF)


def after(value, *others):
    return lax.optimization_barrier((value, *others))[0]


def gather_z(array):
    return lax.all_gather(array, "z", tiled=False)


def sum_z(array):
    return lax.psum_scatter(array, "z", scatter_dimension=0, tiled=False)


def back_to_tokens(pos, total, start):
    pieces = exchange(call(split_kernel, pos, [total], [bf(TOK, DS)] * NY), "y", NY)
    return call(finish_kernel, pos, [*pieces, start], bf(TOK, D))


def spread_weights(piece):
    own = jnp.stack(everywhere(piece, "x", NX))
    return own, shift(own, "c", NC, 1)


def weight_grad_parts(up, pos, mids, slots):
    tail = (HS, F) if up else (F, HS)
    return call(
        functools.partial(weight_grad_kernel, up),
        pos,
        [*mids, slots],
        [bf(NX, EPD, *tail)] * 2,
        flops=7_000_000_000,
    )


def weight_grad(keep, give):
    total = add(keep, shift(give, "c", NC, 1))
    return total, exchange([total[k] for k in range(NX)], "x", NX)


def total_of(arrays):
    return functools.reduce(lambda a, b: a + b, [a.astype(F32) for a in arrays]).astype(BF)


def per_device(tokens, routes, gates, cotangent, w_up, w_down):
    z, x, y, c = (lax.axis_index(name) for name in ("z", "x", "y", "c"))
    pos = jnp.stack([z, x, y, c]).astype(jnp.int32)
    sends = call(
        pack_kernel,
        pos,
        [routes.T, gates.T, tokens, cotangent],
        [bf(TOK + TAB, DS)] * NY + [bf(TOK, DS)] * NY,
        flops=4_000_000_000,
    )
    relaid = exchange(sends[:NY], "y", NY)
    start = call(merge_kernel, pos, relaid, bf(ZT + TAB, DS))
    rows = gather_z(start)
    relaid = exchange(after(list(sends[NY:]), start), "y", NY)
    grad_start = call(merge_plain_kernel, pos, relaid, bf(ZT, DS))
    grads_in = gather_z(grad_start)

    at = y * NC + c
    up = spread_weights(after(lax.dynamic_slice_in_dim(w_up, at * HS, HS, 1), grad_start))
    down = everywhere(after(lax.dynamic_slice_in_dim(w_down, at * HS, HS, 2), grad_start), "x", NX)
    rows = after(rows, *up)

    part = [bf(EPD, ROWS, F)] * NY
    slots, p0, p1, p2, p3, gate, targets, hots = call(
        token_kernel,
        pos,
        [rows, *up],
        [bf(EZ, ROWS, DS), *part, f32(EPD, ROWS, F), f32(NZ, SL), bf(NZ, SL, ZT)],
        flops=13_000_000_000,
    )
    down = jnp.stack(after(down, p0))
    down = (down, shift(down, "c", NC, 1))
    pre = exchange([p0, p1, p2, p3], "y", NY)
    hidden, slope = call(hidden_kernel, pos, [*pre, gate], [bf(EPD, ROWS, F), f32(EPD, ROWS, F)])
    hidden = everywhere(hidden, "y", NY)
    outs = bf(NZ, ZT, DS)
    work = [VM((EZ, ROWS, DS), BF)]
    mixed = call(
        functools.partial(combine_kernel, False), pos, [*hidden, targets, *down], outs, work, flops=8_000_000_000
    )
    grad_slots, p0, p1, p2, p3 = call(
        cotangent_kernel,
        pos,
        [after(grads_in, mixed), hots, *down],
        [bf(EZ, ROWS, DS), *part],
        flops=11_000_000_000,
    )
    mixed = sum_z(mixed)
    grads = exchange([p0, p1, p2, p3], "y", NY)
    keep, give = weight_grad_parts(False, pos, hidden, grad_slots)
    grad_pre = everywhere(call(grad_pre_kernel, pos, [*grads, slope], bf(EPD, ROWS, F)), "y", NY)
    down_total, down_parts = weight_grad(keep, give)
    grad_pre = after(grad_pre, keep)
    token_grad = call(
        functools.partial(combine_kernel, True), pos, [*grad_pre, targets, *up], outs, work, flops=8_000_000_000
    )
    _, up_parts = weight_grad(*weight_grad_parts(True, pos, after(grad_pre, token_grad, down_total), slots))
    token_grad = sum_z(token_grad)
    mixed = back_to_tokens(pos, mixed, tokens)
    up_grad, down_grad = total_of(up_parts), total_of(down_parts)
    token_grad = back_to_tokens(pos, after(token_grad, up_grad, down_grad, mixed), cotangent)
    return mixed, token_grad, up_grad, down_grad


def solution(mesh):
    inner = Mesh(mesh.devices.reshape(NZ, NX, NY, NC), ("z", "x", "y", "c"))
    rows = P(("z", "x", "y", "c"), None)
    experts = P(("z", "x"), None, None)
    return jax.shard_map(
        per_device,
        mesh=inner,
        in_specs=(rows, rows, rows, rows, experts, experts),
        out_specs=(rows, rows, P(("z", "x"), ("y", "c"), None), P(("z", "x"), None, ("y", "c"))),
        check_vma=False,
    )
```

```python
import functools

import jax
import jax.numpy as jnp
from jax import lax
from jax.experimental import pallas as pl
from jax.experimental.pallas import tpu as pltpu
from jax.sharding import Mesh, PartitionSpec as P

BF = jnp.bfloat16
F32 = jnp.float32
COEF = 0.7978845608028654
CUBIC = 0.044715
NZ, NX, NY, NC = 8, 4, 4, 2
TOK, TOP, CAP, D, F = 128, 8, 4, 2048, 128
EPD = 8
EZ = EPD * NX
DS = D // NY
HS = DS // NC
ZT = NY * TOK
SL = EZ * NY * CAP
ROWS = NZ * NY * CAP
TAB = 16
VM = pltpu.VMEM
SM = pltpu.SMEM


def mm(a, b, ca=1, cb=0):
    return lax.dot_general(a, b, (((ca,), (cb,)), ((), ())), preferred_element_type=F32)


def call(body, pos, inputs, outs, scratch=(), flops=2_300_000_000):
    single = not isinstance(outs, (list, tuple))
    shapes = [outs] if single else list(outs)
    moved = sum(a.size * a.dtype.itemsize for a in list(inputs) + shapes)
    result = pl.pallas_call(
        body,
        out_shape=tuple(shapes),
        in_specs=[pl.BlockSpec(memory_space=SM)] + [pl.BlockSpec(memory_space=VM)] * len(inputs),
        out_specs=tuple(pl.BlockSpec(memory_space=VM) for _ in shapes),
        scratch_shapes=list(scratch),
        compiler_params=pltpu.CompilerParams(vmem_limit_bytes=56 * 1024 * 1024),
        cost_estimate=pl.CostEstimate(flops=flops, bytes_accessed=moved, transcendentals=0),
    )(pos, *inputs)
    return result[0] if single else result


def bf(*dims):
    return jax.ShapeDtypeStruct(dims, BF)


def f32(*dims):
    return jax.ShapeDtypeStruct(dims, F32)


def block(index, size):
    return pl.ds(pl.multiple_of(index * size, size), size)


def pack_kernel(pos, routes, gates, tokens, cotangent, *sends):
    y = pos[2]
    lanes = EZ * CAP
    lane = lax.broadcasted_iota(jnp.int32, (1, lanes), 1)
    expert_of = (lane // CAP).astype(F32)
    rank_of = (lane % CAP).astype(F32)
    row = lax.broadcasted_iota(jnp.int32, (TOK, TOK), 0)
    col = lax.broadcasted_iota(jnp.int32, (TOK, TOK), 1)
    before = jnp.where(col < row, 1.0, 0.0).astype(BF)
    token = lax.broadcasted_iota(jnp.int32, (TOK, lanes), 0).astype(F32) + 1.0
    chosen_expert = routes[...].astype(F32).T
    weight_of = gates[...].T
    tids, weights = [], []
    for z in range(NZ):
        named = jnp.zeros((TOK, lanes), F32)
        weight = jnp.zeros((TOK, lanes), F32)
        for k in range(TOP):
            same = chosen_expert[:, k : k + 1] == expert_of + float(z * EZ)
            named = jnp.where(same, 1.0, named)
            weight = jnp.where(same, weight_of[:, k : k + 1], weight)
        rank = mm(before, named.astype(BF))
        kept = (named > 0.0) & (rank == rank_of)
        tids.append(jnp.sum(jnp.where(kept, token, 0.0), axis=0, keepdims=True))
        weights.append(jnp.sum(jnp.where(kept, weight, 0.0), axis=0, keepdims=True))
    table = jnp.concatenate(tids + weights, axis=0).astype(BF)
    for k in range(NY):
        part = block(lax.rem(y + k, NY), DS)
        sends[k][0:TOK, :] = tokens[:, part]
        sends[k][TOK : TOK + TAB, :] = jnp.concatenate([table, jnp.zeros((TAB, DS - lanes), BF)], axis=1)
        sends[NY + k][...] = cotangent[:, part]


def merge_kernel(pos, r0, r1, r2, r3, out):
    y = pos[2]
    lanes = EZ * CAP
    near = lax.broadcasted_iota(jnp.int32, (lanes, SL), 0)
    far = lax.broadcasted_iota(jnp.int32, (lanes, SL), 1)
    table = jnp.zeros((TAB, SL), F32)
    for k, r in enumerate((r0, r1, r2, r3)):
        q = lax.rem(y - k + NY, NY)
        out[block(q, TOK), :] = r[0:TOK, :]
        spread = jnp.where(far == (near // CAP) * (NY * CAP) + q * CAP + near % CAP, 1.0, 0.0).astype(BF)
        table = table + mm(r[TOK : TOK + TAB, 0:lanes], spread)
    out[ZT : ZT + TAB, :] = table.astype(BF)


def merge_plain_kernel(pos, r0, r1, r2, r3, out):
    y = pos[2]
    for k, r in enumerate((r0, r1, r2, r3)):
        out[block(lax.rem(y - k + NY, NY), TOK), :] = r[...]


def first_layer(turned, pos, slots, own, other, parts):
    x, y, c = pos[1], pos[2], pos[3]
    cb = 1 if turned else 0
    mine, theirs = block(c, HS), block(1 - c, HS)
    for k in range(NY):
        q = lax.rem(y + k, NY)
        kx = lax.rem(x - q + NX, NX)
        for le in range(EPD):
            e = q * EPD + le
            total = mm(slots[e, :, mine], own[kx, le], 1, cb) + mm(slots[e, :, theirs], other[kx, le], 1, cb)
            parts[k][le] = total.astype(BF)


def token_kernel(pos, sources, own, other, slots, p0, p1, p2, p3, gate, targets, hots):
    z, y = pos[0], pos[2]
    kind = lax.broadcasted_iota(jnp.int32, (TAB, 128), 0)
    pick_token = jnp.where(kind == z, 1.0, 0.0).astype(BF)
    pick_gate = jnp.where(kind == z + 8, 1.0, 0.0).astype(BF)
    slot = lax.broadcasted_iota(jnp.int32, (SL, 128), 0)
    base = ((slot // CAP) % NY * TOK - 1).astype(F32)
    lane = lax.broadcasted_iota(jnp.int32, (SL, 128), 1).astype(F32)
    slot_lane = lax.broadcasted_iota(jnp.int32, (1, SL), 1)
    base_lane = ((slot_lane // CAP) % NY * TOK - 1).astype(F32)
    plane = lax.broadcasted_iota(jnp.int32, (TAB, SL), 0)
    for s in range(NZ):
        rows = sources.at[s]
        table = rows[ZT : ZT + TAB, :]
        token = mm(table, pick_token, 0, 0)
        target = jnp.where(token > 0.0, token + base, -1.0)
        hot = jnp.concatenate(
            [jnp.where(target == lane + float(128 * j), 1.0, 0.0).astype(BF) for j in range(NY)], axis=1
        )
        hots[s] = hot
        got = mm(hot, rows[0:ZT, :]).astype(BF)
        slots[:, s * 16 : (s + 1) * 16, :] = got.reshape(EZ, 16, DS)
        token_row = jnp.sum(jnp.where(plane == z, table.astype(F32), 0.0), axis=0, keepdims=True)
        targets[s : s + 1, :] = jnp.where(token_row > 0.0, token_row + base_lane, -1.0)
        weight = mm(rows[ZT : ZT + TAB, block(y, 128)], pick_gate, 0, 0)
        gate[:, s * 16 : (s + 1) * 16, :] = weight.reshape(EPD, 16, 128)
    first_layer(False, pos, slots, own, other, (p0, p1, p2, p3))


def cotangent_kernel(pos, sources, hots, own, other, slots, p0, p1, p2, p3):
    for s in range(NZ):
        got = mm(hots[s], sources[s]).astype(BF)
        slots[:, s * 16 : (s + 1) * 16, :] = got.reshape(EZ, 16, DS)
    first_layer(True, pos, slots, own, other, (p0, p1, p2, p3))


def hidden_kernel(pos, r0, r1, r2, r3, gate, hidden, slope):
    for e in range(EPD):
        pre = (r0[e].astype(F32) + r1[e].astype(F32)) + (r2[e].astype(F32) + r3[e].astype(F32))
        square = pre * pre
        inner = jnp.tanh(COEF * (pre + CUBIC * square * pre))
        weight = gate[e]
        hidden[e] = (weight * (0.5 * pre * (1.0 + inner))).astype(BF)
        slope[e] = weight * (
            0.5 * (1.0 + inner) + 0.5 * pre * (1.0 - inner * inner) * COEF * (1.0 + 3.0 * CUBIC * square)
        )


def grad_pre_kernel(pos, r0, r1, r2, r3, slope, out):
    for e in range(EPD):
        grad = (r0[e].astype(F32) + r1[e].astype(F32)) + (r2[e].astype(F32) + r3[e].astype(F32))
        out[e] = (grad * slope[e]).astype(BF)


def combine_kernel(turned, pos, h0, h1, h2, h3, targets, own, other, out, outs):
    x, y, c = pos[1], pos[2], pos[3]
    cb = 1 if turned else 0
    mine, theirs = block(c, HS), block(1 - c, HS)
    for k, h in enumerate((h0, h1, h2, h3)):
        q = lax.rem(y - k + NY, NY)
        kx = lax.rem(x - q + NX, NX)
        for le in range(EPD):
            e = q * EPD + le
            outs[e, :, mine] = mm(h[le], own[kx, le], 1, cb).astype(BF)
            outs[e, :, theirs] = mm(h[le], other[kx, le], 1, cb).astype(BF)
    row = lax.broadcasted_iota(jnp.int32, (ZT, SL), 0).astype(F32)
    for s in range(NZ):
        hot = jnp.where(targets[s : s + 1, :] == row, 1.0, 0.0).astype(BF)
        out[s] = mm(hot, outs[:, s * 16 : (s + 1) * 16, :].reshape(SL, DS)).astype(BF)


def weight_grad_kernel(up, pos, h0, h1, h2, h3, slots, keep, give):
    x, y, c = pos[1], pos[2], pos[3]
    for k, h in enumerate((h0, h1, h2, h3)):
        q = lax.rem(y - k + NY, NY)
        kx = lax.rem(q - x + NX, NX)
        for le in range(EPD):
            for out, half in ((keep, c), (give, 1 - c)):
                rows = slots[q * EPD + le, :, block(half, HS)]
                grad = mm(rows, h[le], 0, 0) if up else mm(h[le], rows, 0, 0)
                out[kx, le] = grad.astype(BF)


def split_kernel(pos, total, s0, s1, s2, s3):
    y = pos[2]
    for k, out in enumerate((s0, s1, s2, s3)):
        out[...] = total[block(lax.rem(y + k, NY), TOK), :]


def finish_kernel(pos, r0, r1, r2, r3, start, out):
    y = pos[2]
    for k, r in enumerate((r0, r1, r2, r3)):
        part = block(lax.rem(y - k + NY, NY), DS)
        out[:, part] = (start[:, part].astype(F32) + r[...].astype(F32)).astype(BF)


def shift(array, axis, size, by):
    return lax.ppermute(array, axis, [(i, (i + by) % size) for i in range(size)])


def everywhere(array, axis, size):
    return [array] + [shift(array, axis, size, k) for k in range(1, size)]


def exchange(arrays, axis, size):
    return [arrays[0]] + [shift(arrays[k], axis, size, k) for k in range(1, size)]


def add(a, b):
    return (a.astype(F32) + b.astype(F32)).astype(BF)


def after(value, *others):
    return lax.optimization_barrier((value, *others))[0]


def gather_z(array):
    return lax.all_gather(array, "z", tiled=False)


def sum_z(array):
    return lax.psum_scatter(array, "z", scatter_dimension=0, tiled=False)


def back_to_tokens(pos, total, start):
    pieces = exchange(call(split_kernel, pos, [total], [bf(TOK, DS)] * NY), "y", NY)
    return call(finish_kernel, pos, [*pieces, start], bf(TOK, D))


def spread_weights(piece):
    own = jnp.stack(everywhere(piece, "x", NX))
    return own, shift(own, "c", NC, 1)


def weight_grad_parts(up, pos, mids, slots):
    tail = (HS, F) if up else (F, HS)
    return call(
        functools.partial(weight_grad_kernel, up),
        pos,
        [*mids, slots],
        [bf(NX, EPD, *tail)] * 2,
        flops=7_000_000_000,
    )


def weight_grad(keep, give):
    total = add(keep, shift(give, "c", NC, 1))
    return total, exchange([total[k] for k in range(NX)], "x", NX)


def total_of(arrays):
    return functools.reduce(lambda a, b: a + b, [a.astype(F32) for a in arrays]).astype(BF)


def per_device(tokens, routes, gates, cotangent, w_up, w_down):
    z, x, y, c = (lax.axis_index(name) for name in ("z", "x", "y", "c"))
    pos = jnp.stack([z, x, y, c]).astype(jnp.int32)
    sends = call(
        pack_kernel,
        pos,
        [routes.T, gates.T, tokens, cotangent],
        [bf(TOK + TAB, DS)] * NY + [bf(TOK, DS)] * NY,
        flops=4_000_000_000,
    )
    relaid = exchange(sends[:NY], "y", NY)
    start = call(merge_kernel, pos, relaid, bf(ZT + TAB, DS))
    rows = gather_z(start)
    relaid = exchange(after(list(sends[NY:]), start), "y", NY)
    grad_start = call(merge_plain_kernel, pos, relaid, bf(ZT, DS))
    grads_in = gather_z(grad_start)

    at = y * NC + c
    up = spread_weights(after(lax.dynamic_slice_in_dim(w_up, at * HS, HS, 1), grad_start))
    down = everywhere(after(lax.dynamic_slice_in_dim(w_down, at * HS, HS, 2), grad_start), "x", NX)
    rows = after(rows, *up)

    part = [bf(EPD, ROWS, F)] * NY
    slots, p0, p1, p2, p3, gate, targets, hots = call(
        token_kernel,
        pos,
        [rows, *up],
        [bf(EZ, ROWS, DS), *part, f32(EPD, ROWS, F), f32(NZ, SL), bf(NZ, SL, ZT)],
        flops=13_000_000_000,
    )
    down = jnp.stack(after(down, p0))
    down = (down, shift(down, "c", NC, 1))
    pre = exchange([p0, p1, p2, p3], "y", NY)
    hidden, slope = call(hidden_kernel, pos, [*pre, gate], [bf(EPD, ROWS, F), f32(EPD, ROWS, F)])
    hidden = everywhere(hidden, "y", NY)
    outs = bf(NZ, ZT, DS)
    work = [VM((EZ, ROWS, DS), BF)]
    mixed = call(
        functools.partial(combine_kernel, False), pos, [*hidden, targets, *down], outs, work, flops=8_000_000_000
    )
    grad_slots, p0, p1, p2, p3 = call(
        cotangent_kernel,
        pos,
        [after(grads_in, mixed), hots, *down],
        [bf(EZ, ROWS, DS), *part],
        flops=11_000_000_000,
    )
    mixed = sum_z(mixed)
    grads = exchange([p0, p1, p2, p3], "y", NY)
    keep, give = weight_grad_parts(False, pos, hidden, grad_slots)
    grad_pre = everywhere(call(grad_pre_kernel, pos, [*grads, slope], bf(EPD, ROWS, F)), "y", NY)
    down_total, down_parts = weight_grad(keep, give)
    grad_pre = after(grad_pre, keep)
    token_grad = call(
        functools.partial(combine_kernel, True), pos, [*grad_pre, targets, *up], outs, work, flops=8_000_000_000
    )
    _, up_parts = weight_grad(*weight_grad_parts(True, pos, after(grad_pre, token_grad), slots))
    token_grad = sum_z(token_grad)
    mixed = back_to_tokens(pos, mixed, tokens)
    down_grad = total_of(after(down_parts, mixed))
    up_grad = total_of(after(up_parts, mixed))
    token_grad = back_to_tokens(pos, after(token_grad, up_grad, down_grad, mixed), cotangent)
    return mixed, token_grad, up_grad, down_grad


def solution(mesh):
    inner = Mesh(mesh.devices.reshape(NZ, NX, NY, NC), ("z", "x", "y", "c"))
    rows = P(("z", "x", "y", "c"), None)
    experts = P(("z", "x"), None, None)
    return jax.shard_map(
        per_device,
        mesh=inner,
        in_specs=(rows, rows, rows, rows, experts, experts),
        out_specs=(rows, rows, P(("z", "x"), ("y", "c"), None), P(("z", "x"), None, ("y", "c"))),
        check_vma=False,
    )
```

```python
import functools

import jax
import jax.numpy as jnp
from jax import lax
from jax.experimental import pallas as pl
from jax.experimental.pallas import tpu as pltpu
from jax.sharding import Mesh, PartitionSpec as P

BF = jnp.bfloat16
F32 = jnp.float32
COEF = 0.7978845608028654
CUBIC = 0.044715
NZ, NX, NY, NC = 8, 4, 4, 2
TOK, TOP, CAP, D, F = 128, 8, 4, 2048, 128
EPD = 8
EZ = EPD * NX
DS = D // NY
HS = DS // NC
ZT = NY * TOK
SL = EZ * NY * CAP
ROWS = NZ * NY * CAP
TAB = 16
VM = pltpu.VMEM
SM = pltpu.SMEM


def mm(a, b, ca=1, cb=0):
    return lax.dot_general(a, b, (((ca,), (cb,)), ((), ())), preferred_element_type=F32)


def call(body, pos, inputs, outs, scratch=(), flops=2_300_000_000):
    single = not isinstance(outs, (list, tuple))
    shapes = [outs] if single else list(outs)
    moved = sum(a.size * a.dtype.itemsize for a in list(inputs) + shapes)
    result = pl.pallas_call(
        body,
        out_shape=tuple(shapes),
        in_specs=[pl.BlockSpec(memory_space=SM)] + [pl.BlockSpec(memory_space=VM)] * len(inputs),
        out_specs=tuple(pl.BlockSpec(memory_space=VM) for _ in shapes),
        scratch_shapes=list(scratch),
        compiler_params=pltpu.CompilerParams(vmem_limit_bytes=56 * 1024 * 1024),
        cost_estimate=pl.CostEstimate(flops=flops, bytes_accessed=moved, transcendentals=0),
    )(pos, *inputs)
    return result[0] if single else result


def bf(*dims):
    return jax.ShapeDtypeStruct(dims, BF)


def f32(*dims):
    return jax.ShapeDtypeStruct(dims, F32)


def block(index, size):
    return pl.ds(pl.multiple_of(index * size, size), size)


def pack_kernel(pos, routes, gates, tokens, cotangent, *sends):
    y = pos[2]
    lanes = EZ * CAP
    lane = lax.broadcasted_iota(jnp.int32, (1, lanes), 1)
    expert_of = (lane // CAP).astype(F32)
    rank_of = (lane % CAP).astype(F32)
    row = lax.broadcasted_iota(jnp.int32, (TOK, TOK), 0)
    col = lax.broadcasted_iota(jnp.int32, (TOK, TOK), 1)
    before = jnp.where(col < row, 1.0, 0.0).astype(BF)
    token = lax.broadcasted_iota(jnp.int32, (TOK, lanes), 0).astype(F32) + 1.0
    chosen_expert = routes[...].astype(F32).T
    weight_of = gates[...].T
    tids, weights = [], []
    for z in range(NZ):
        named = jnp.zeros((TOK, lanes), F32)
        weight = jnp.zeros((TOK, lanes), F32)
        for k in range(TOP):
            same = chosen_expert[:, k : k + 1] == expert_of + float(z * EZ)
            named = jnp.where(same, 1.0, named)
            weight = jnp.where(same, weight_of[:, k : k + 1], weight)
        rank = mm(before, named.astype(BF))
        kept = (named > 0.0) & (rank == rank_of)
        tids.append(jnp.sum(jnp.where(kept, token, 0.0), axis=0, keepdims=True))
        weights.append(jnp.sum(jnp.where(kept, weight, 0.0), axis=0, keepdims=True))
    table = jnp.concatenate(tids + weights, axis=0).astype(BF)
    for k in range(NY):
        part = block(lax.rem(y + k, NY), DS)
        sends[k][0:TOK, :] = tokens[:, part]
        sends[k][TOK : TOK + TAB, :] = jnp.concatenate([table, jnp.zeros((TAB, DS - lanes), BF)], axis=1)
        sends[NY + k][...] = cotangent[:, part]


def merge_kernel(pos, r0, r1, r2, r3, out):
    y = pos[2]
    lanes = EZ * CAP
    near = lax.broadcasted_iota(jnp.int32, (lanes, SL), 0)
    far = lax.broadcasted_iota(jnp.int32, (lanes, SL), 1)
    table = jnp.zeros((TAB, SL), F32)
    for k, r in enumerate((r0, r1, r2, r3)):
        q = lax.rem(y - k + NY, NY)
        out[block(q, TOK), :] = r[0:TOK, :]
        spread = jnp.where(far == (near // CAP) * (NY * CAP) + q * CAP + near % CAP, 1.0, 0.0).astype(BF)
        table = table + mm(r[TOK : TOK + TAB, 0:lanes], spread)
    out[ZT : ZT + TAB, :] = table.astype(BF)


def merge_plain_kernel(pos, r0, r1, r2, r3, out):
    y = pos[2]
    for k, r in enumerate((r0, r1, r2, r3)):
        out[block(lax.rem(y - k + NY, NY), TOK), :] = r[...]


def first_layer(turned, pos, slots, own, other, parts):
    x, y, c = pos[1], pos[2], pos[3]
    cb = 1 if turned else 0
    mine, theirs = block(c, HS), block(1 - c, HS)
    for k in range(NY):
        q = lax.rem(y + k, NY)
        kx = lax.rem(x - q + NX, NX)
        for le in range(EPD):
            e = q * EPD + le
            total = mm(slots[e, :, mine], own[kx, le], 1, cb) + mm(slots[e, :, theirs], other[kx, le], 1, cb)
            parts[k][le] = total.astype(BF)


def token_kernel(pos, sources, own, other, slots, p0, p1, p2, p3, gate, targets, hots):
    z, y = pos[0], pos[2]
    kind = lax.broadcasted_iota(jnp.int32, (TAB, 128), 0)
    pick_token = jnp.where(kind == z, 1.0, 0.0).astype(BF)
    pick_gate = jnp.where(kind == z + 8, 1.0, 0.0).astype(BF)
    slot = lax.broadcasted_iota(jnp.int32, (SL, 128), 0)
    base = ((slot // CAP) % NY * TOK - 1).astype(F32)
    lane = lax.broadcasted_iota(jnp.int32, (SL, 128), 1).astype(F32)
    slot_lane = lax.broadcasted_iota(jnp.int32, (1, SL), 1)
    base_lane = ((slot_lane // CAP) % NY * TOK - 1).astype(F32)
    plane = lax.broadcasted_iota(jnp.int32, (TAB, SL), 0)
    for s in range(NZ):
        rows = sources.at[s]
        table = rows[ZT : ZT + TAB, :]
        token = mm(table, pick_token, 0, 0)
        target = jnp.where(token > 0.0, token + base, -1.0)
        hot = jnp.concatenate(
            [jnp.where(target == lane + float(128 * j), 1.0, 0.0).astype(BF) for j in range(NY)], axis=1
        )
        hots[s] = hot
        got = mm(hot, rows[0:ZT, :]).astype(BF)
        slots[:, s * 16 : (s + 1) * 16, :] = got.reshape(EZ, 16, DS)
        token_row = jnp.sum(jnp.where(plane == z, table.astype(F32), 0.0), axis=0, keepdims=True)
        targets[s : s + 1, :] = jnp.where(token_row > 0.0, token_row + base_lane, -1.0)
        weight = mm(rows[ZT : ZT + TAB, block(y, 128)], pick_gate, 0, 0)
        gate[:, s * 16 : (s + 1) * 16, :] = weight.reshape(EPD, 16, 128)
    first_layer(False, pos, slots, own, other, (p0, p1, p2, p3))


def cotangent_kernel(pos, sources, hots, own, other, slots, p0, p1, p2, p3):
    for s in range(NZ):
        got = mm(hots[s], sources[s]).astype(BF)
        slots[:, s * 16 : (s + 1) * 16, :] = got.reshape(EZ, 16, DS)
    first_layer(True, pos, slots, own, other, (p0, p1, p2, p3))


def hidden_kernel(pos, r0, r1, r2, r3, gate, hidden, slope):
    for e in range(EPD):
        pre = (r0[e].astype(F32) + r1[e].astype(F32)) + (r2[e].astype(F32) + r3[e].astype(F32))
        square = pre * pre
        inner = jnp.tanh(COEF * (pre + CUBIC * square * pre))
        weight = gate[e]
        hidden[e] = (weight * (0.5 * pre * (1.0 + inner))).astype(BF)
        slope[e] = weight * (
            0.5 * (1.0 + inner) + 0.5 * pre * (1.0 - inner * inner) * COEF * (1.0 + 3.0 * CUBIC * square)
        )


def grad_pre_kernel(pos, r0, r1, r2, r3, slope, out):
    for e in range(EPD):
        grad = (r0[e].astype(F32) + r1[e].astype(F32)) + (r2[e].astype(F32) + r3[e].astype(F32))
        out[e] = (grad * slope[e]).astype(BF)


def combine_kernel(turned, pos, h0, h1, h2, h3, targets, own, other, out, outs):
    x, y, c = pos[1], pos[2], pos[3]
    cb = 1 if turned else 0
    mine, theirs = block(c, HS), block(1 - c, HS)
    for k, h in enumerate((h0, h1, h2, h3)):
        q = lax.rem(y - k + NY, NY)
        kx = lax.rem(x - q + NX, NX)
        for le in range(EPD):
            e = q * EPD + le
            outs[e, :, mine] = mm(h[le], own[kx, le], 1, cb).astype(BF)
            outs[e, :, theirs] = mm(h[le], other[kx, le], 1, cb).astype(BF)
    row = lax.broadcasted_iota(jnp.int32, (ZT, SL), 0).astype(F32)
    for s in range(NZ):
        hot = jnp.where(targets[s : s + 1, :] == row, 1.0, 0.0).astype(BF)
        out[s] = mm(hot, outs[:, s * 16 : (s + 1) * 16, :].reshape(SL, DS)).astype(BF)


def weight_grad_kernel(up, pos, h0, h1, h2, h3, slots, keep, give):
    x, y, c = pos[1], pos[2], pos[3]
    for k, h in enumerate((h0, h1, h2, h3)):
        q = lax.rem(y - k + NY, NY)
        kx = lax.rem(q - x + NX, NX)
        for le in range(EPD):
            for out, half in ((keep, c), (give, 1 - c)):
                rows = slots[q * EPD + le, :, block(half, HS)]
                grad = mm(rows, h[le], 0, 0) if up else mm(h[le], rows, 0, 0)
                out[kx, le] = grad.astype(BF)


def split_kernel(pos, total, s0, s1, s2, s3):
    y = pos[2]
    for k, out in enumerate((s0, s1, s2, s3)):
        out[...] = total[block(lax.rem(y + k, NY), TOK), :]


def finish_kernel(pos, r0, r1, r2, r3, start, out):
    y = pos[2]
    for k, r in enumerate((r0, r1, r2, r3)):
        part = block(lax.rem(y - k + NY, NY), DS)
        out[:, part] = (start[:, part].astype(F32) + r[...].astype(F32)).astype(BF)


def shift(array, axis, size, by):
    return lax.ppermute(array, axis, [(i, (i + by) % size) for i in range(size)])


def everywhere(array, axis, size):
    return [array] + [shift(array, axis, size, k) for k in range(1, size)]


def exchange(arrays, axis, size):
    return [arrays[0]] + [shift(arrays[k], axis, size, k) for k in range(1, size)]


def add(a, b):
    return (a.astype(F32) + b.astype(F32)).astype(BF)


def after(value, *others):
    return lax.optimization_barrier((value, *others))[0]


def gather_z(array):
    return lax.all_gather(array, "z", tiled=False)


def sum_z(array):
    return lax.psum_scatter(array, "z", scatter_dimension=0, tiled=False)


def back_to_tokens(pos, total):
    return exchange(call(split_kernel, pos, [total], [bf(TOK, DS)] * NY), "y", NY)


def spread_weights(piece):
    own = jnp.stack(everywhere(piece, "x", NX))
    return own, shift(own, "c", NC, 1)


def weight_grad_parts(up, pos, mids, slots):
    tail = (HS, F) if up else (F, HS)
    return call(
        functools.partial(weight_grad_kernel, up),
        pos,
        [*mids, slots],
        [bf(NX, EPD, *tail)] * 2,
        flops=7_000_000_000,
    )


def weight_grad(keep, give):
    total = add(keep, shift(give, "c", NC, 1))
    return total, exchange([total[k] for k in range(NX)], "x", NX)


def total_of(arrays):
    return functools.reduce(lambda a, b: a + b, [a.astype(F32) for a in arrays]).astype(BF)


def per_device(tokens, routes, gates, cotangent, w_up, w_down):
    z, x, y, c = (lax.axis_index(name) for name in ("z", "x", "y", "c"))
    pos = jnp.stack([z, x, y, c]).astype(jnp.int32)
    sends = call(
        pack_kernel,
        pos,
        [routes.T, gates.T, tokens, cotangent],
        [bf(TOK + TAB, DS)] * NY + [bf(TOK, DS)] * NY,
        flops=4_000_000_000,
    )
    relaid = exchange(sends[:NY], "y", NY)
    start = call(merge_kernel, pos, relaid, bf(ZT + TAB, DS))
    rows = gather_z(start)
    relaid = exchange(after(list(sends[NY:]), start), "y", NY)
    grad_start = call(merge_plain_kernel, pos, relaid, bf(ZT, DS))
    grads_in = gather_z(grad_start)

    at = y * NC + c
    up = spread_weights(after(lax.dynamic_slice_in_dim(w_up, at * HS, HS, 1), grad_start))
    down = everywhere(after(lax.dynamic_slice_in_dim(w_down, at * HS, HS, 2), grad_start), "x", NX)
    rows = after(rows, *up)

    part = [bf(EPD, ROWS, F)] * NY
    slots, p0, p1, p2, p3, gate, targets, hots = call(
        token_kernel,
        pos,
        [rows, *up],
        [bf(EZ, ROWS, DS), *part, f32(EPD, ROWS, F), f32(NZ, SL), bf(NZ, SL, ZT)],
        flops=13_000_000_000,
    )
    down = jnp.stack(after(down, p0))
    down = (down, shift(down, "c", NC, 1))
    pre = exchange([p0, p1, p2, p3], "y", NY)
    hidden, slope = call(hidden_kernel, pos, [*pre, gate], [bf(EPD, ROWS, F), f32(EPD, ROWS, F)])
    hidden = everywhere(hidden, "y", NY)
    outs = bf(NZ, ZT, DS)
    work = [VM((EZ, ROWS, DS), BF)]
    mixed = call(
        functools.partial(combine_kernel, False), pos, [*hidden, targets, *down], outs, work, flops=8_000_000_000
    )
    grad_slots, p0, p1, p2, p3 = call(
        cotangent_kernel,
        pos,
        [after(grads_in, mixed), hots, *down],
        [bf(EZ, ROWS, DS), *part],
        flops=11_000_000_000,
    )
    mixed = sum_z(mixed)
    grads = exchange([p0, p1, p2, p3], "y", NY)
    keep, give = weight_grad_parts(False, pos, hidden, grad_slots)
    grad_pre = everywhere(call(grad_pre_kernel, pos, [*grads, slope], bf(EPD, ROWS, F)), "y", NY)
    down_total, down_parts = weight_grad(keep, give)
    grad_pre = after(grad_pre, keep)
    token_grad = call(
        functools.partial(combine_kernel, True), pos, [*grad_pre, targets, *up], outs, work, flops=8_000_000_000
    )
    _, up_parts = weight_grad(*weight_grad_parts(True, pos, after(grad_pre, token_grad, down_total), slots))
    token_grad = sum_z(token_grad)
    mixed = back_to_tokens(pos, mixed)
    down_grad = total_of(down_parts)
    token_grad = back_to_tokens(pos, after(token_grad, up_parts, down_grad, mixed))
    up_grad = total_of(up_parts)
    mixed = call(finish_kernel, pos, [*mixed, tokens], bf(TOK, D))
    token_grad = call(finish_kernel, pos, [*token_grad, cotangent], bf(TOK, D))
    return mixed, token_grad, up_grad, down_grad


def solution(mesh):
    inner = Mesh(mesh.devices.reshape(NZ, NX, NY, NC), ("z", "x", "y", "c"))
    rows = P(("z", "x", "y", "c"), None)
    experts = P(("z", "x"), None, None)
    return jax.shard_map(
        per_device,
        mesh=inner,
        in_specs=(rows, rows, rows, rows, experts, experts),
        out_specs=(rows, rows, P(("z", "x"), ("y", "c"), None), P(("z", "x"), None, ("y", "c"))),
        check_vma=False,
    )
```

```python
import functools

import jax
import jax.numpy as jnp
from jax import lax
from jax.experimental import pallas as pl
from jax.experimental.pallas import tpu as pltpu
from jax.sharding import Mesh, PartitionSpec as P

BF = jnp.bfloat16
F32 = jnp.float32
COEF = 0.7978845608028654
CUBIC = 0.044715
NZ, NX, NY, NC = 8, 4, 4, 2
TOK, TOP, CAP, D, F = 128, 8, 4, 2048, 128
EPD = 8
EZ = EPD * NX
DS = D // NY
HS = DS // NC
ZT = NY * TOK
SL = EZ * NY * CAP
ROWS = NZ * NY * CAP
TAB = 16
VM = pltpu.VMEM
SM = pltpu.SMEM


def mm(a, b, ca=1, cb=0):
    return lax.dot_general(a, b, (((ca,), (cb,)), ((), ())), preferred_element_type=F32)


def call(body, pos, inputs, outs, scratch=(), flops=2_300_000_000):
    single = not isinstance(outs, (list, tuple))
    shapes = [outs] if single else list(outs)
    moved = sum(a.size * a.dtype.itemsize for a in list(inputs) + shapes)
    result = pl.pallas_call(
        body,
        out_shape=tuple(shapes),
        in_specs=[pl.BlockSpec(memory_space=SM)] + [pl.BlockSpec(memory_space=VM)] * len(inputs),
        out_specs=tuple(pl.BlockSpec(memory_space=VM) for _ in shapes),
        scratch_shapes=list(scratch),
        compiler_params=pltpu.CompilerParams(vmem_limit_bytes=56 * 1024 * 1024),
        cost_estimate=pl.CostEstimate(flops=flops, bytes_accessed=moved, transcendentals=0),
    )(pos, *inputs)
    return result[0] if single else result


def bf(*dims):
    return jax.ShapeDtypeStruct(dims, BF)


def f32(*dims):
    return jax.ShapeDtypeStruct(dims, F32)


def block(index, size):
    return pl.ds(pl.multiple_of(index * size, size), size)


def pack_kernel(pos, routes, gates, tokens, cotangent, *sends):
    y = pos[2]
    lanes = EZ * CAP
    lane = lax.broadcasted_iota(jnp.int32, (1, lanes), 1)
    expert_of = (lane // CAP).astype(F32)
    rank_of = (lane % CAP).astype(F32)
    row = lax.broadcasted_iota(jnp.int32, (TOK, TOK), 0)
    col = lax.broadcasted_iota(jnp.int32, (TOK, TOK), 1)
    before = jnp.where(col < row, 1.0, 0.0).astype(BF)
    token = lax.broadcasted_iota(jnp.int32, (TOK, lanes), 0).astype(F32) + 1.0
    chosen_expert = routes[...].astype(F32).T
    weight_of = gates[...].T
    tids, weights = [], []
    for z in range(NZ):
        named = jnp.zeros((TOK, lanes), F32)
        weight = jnp.zeros((TOK, lanes), F32)
        for k in range(TOP):
            same = chosen_expert[:, k : k + 1] == expert_of + float(z * EZ)
            named = jnp.where(same, 1.0, named)
            weight = jnp.where(same, weight_of[:, k : k + 1], weight)
        rank = mm(before, named.astype(BF))
        kept = (named > 0.0) & (rank == rank_of)
        tids.append(jnp.sum(jnp.where(kept, token, 0.0), axis=0, keepdims=True))
        weights.append(jnp.sum(jnp.where(kept, weight, 0.0), axis=0, keepdims=True))
    table = jnp.concatenate(tids + weights, axis=0).astype(BF)
    for k in range(NY):
        part = block(lax.rem(y + k, NY), DS)
        sends[k][0:TOK, :] = tokens[:, part]
        sends[k][TOK : TOK + TAB, :] = jnp.concatenate([table, jnp.zeros((TAB, DS - lanes), BF)], axis=1)
        sends[NY + k][...] = cotangent[:, part]


def merge_kernel(pos, r0, r1, r2, r3, out):
    y = pos[2]
    lanes = EZ * CAP
    near = lax.broadcasted_iota(jnp.int32, (lanes, SL), 0)
    far = lax.broadcasted_iota(jnp.int32, (lanes, SL), 1)
    table = jnp.zeros((TAB, SL), F32)
    for k, r in enumerate((r0, r1, r2, r3)):
        q = lax.rem(y - k + NY, NY)
        out[block(q, TOK), :] = r[0:TOK, :]
        spread = jnp.where(far == (near // CAP) * (NY * CAP) + q * CAP + near % CAP, 1.0, 0.0).astype(BF)
        table = table + mm(r[TOK : TOK + TAB, 0:lanes], spread)
    out[ZT : ZT + TAB, :] = table.astype(BF)


def merge_plain_kernel(pos, r0, r1, r2, r3, out):
    y = pos[2]
    for k, r in enumerate((r0, r1, r2, r3)):
        out[block(lax.rem(y - k + NY, NY), TOK), :] = r[...]


def first_layer(turned, pos, slots, own, other, parts):
    x, y, c = pos[1], pos[2], pos[3]
    cb = 1 if turned else 0
    mine, theirs = block(c, HS), block(1 - c, HS)
    for k in range(NY):
        q = lax.rem(y + k, NY)
        kx = lax.rem(x - q + NX, NX)
        for le in range(EPD):
            e = q * EPD + le
            total = mm(slots[e, :, mine], own[kx, le], 1, cb) + mm(slots[e, :, theirs], other[kx, le], 1, cb)
            parts[k][le] = total.astype(BF)


def token_kernel(pos, sources, own, other, slots, p0, p1, p2, p3, gate, targets, hots):
    z, y = pos[0], pos[2]
    kind = lax.broadcasted_iota(jnp.int32, (TAB, 128), 0)
    pick_token = jnp.where(kind == z, 1.0, 0.0).astype(BF)
    pick_gate = jnp.where(kind == z + 8, 1.0, 0.0).astype(BF)
    slot = lax.broadcasted_iota(jnp.int32, (SL, 128), 0)
    base = ((slot // CAP) % NY * TOK - 1).astype(F32)
    lane = lax.broadcasted_iota(jnp.int32, (SL, 128), 1).astype(F32)
    slot_lane = lax.broadcasted_iota(jnp.int32, (1, SL), 1)
    base_lane = ((slot_lane // CAP) % NY * TOK - 1).astype(F32)
    plane = lax.broadcasted_iota(jnp.int32, (TAB, SL), 0)
    for s in range(NZ):
        rows = sources.at[s]
        table = rows[ZT : ZT + TAB, :]
        token = mm(table, pick_token, 0, 0)
        target = jnp.where(token > 0.0, token + base, -1.0)
        hot = jnp.concatenate(
            [jnp.where(target == lane + float(128 * j), 1.0, 0.0).astype(BF) for j in range(NY)], axis=1
        )
        hots[s] = hot
        got = mm(hot, rows[0:ZT, :]).astype(BF)
        slots[:, s * 16 : (s + 1) * 16, :] = got.reshape(EZ, 16, DS)
        token_row = jnp.sum(jnp.where(plane == z, table.astype(F32), 0.0), axis=0, keepdims=True)
        targets[s : s + 1, :] = jnp.where(token_row > 0.0, token_row + base_lane, -1.0)
        weight = mm(rows[ZT : ZT + TAB, block(y, 128)], pick_gate, 0, 0)
        gate[:, s * 16 : (s + 1) * 16, :] = weight.reshape(EPD, 16, 128)
    first_layer(False, pos, slots, own, other, (p0, p1, p2, p3))


def cotangent_kernel(pos, sources, hots, own, other, slots, p0, p1, p2, p3):
    for s in range(NZ):
        got = mm(hots[s], sources[s]).astype(BF)
        slots[:, s * 16 : (s + 1) * 16, :] = got.reshape(EZ, 16, DS)
    first_layer(True, pos, slots, own, other, (p0, p1, p2, p3))


def hidden_kernel(pos, r0, r1, r2, r3, gate, hidden, slope):
    for e in range(EPD):
        pre = (r0[e].astype(F32) + r1[e].astype(F32)) + (r2[e].astype(F32) + r3[e].astype(F32))
        square = pre * pre
        inner = jnp.tanh(COEF * (pre + CUBIC * square * pre))
        weight = gate[e]
        hidden[e] = (weight * (0.5 * pre * (1.0 + inner))).astype(BF)
        slope[e] = weight * (
            0.5 * (1.0 + inner) + 0.5 * pre * (1.0 - inner * inner) * COEF * (1.0 + 3.0 * CUBIC * square)
        )


def grad_pre_kernel(pos, r0, r1, r2, r3, slope, out):
    for e in range(EPD):
        grad = (r0[e].astype(F32) + r1[e].astype(F32)) + (r2[e].astype(F32) + r3[e].astype(F32))
        out[e] = (grad * slope[e]).astype(BF)


def combine_kernel(turned, pos, h0, h1, h2, h3, targets, own, other, out, outs):
    x, y, c = pos[1], pos[2], pos[3]
    cb = 1 if turned else 0
    mine, theirs = block(c, HS), block(1 - c, HS)
    for k, h in enumerate((h0, h1, h2, h3)):
        q = lax.rem(y - k + NY, NY)
        kx = lax.rem(x - q + NX, NX)
        for le in range(EPD):
            e = q * EPD + le
            outs[e, :, mine] = mm(h[le], own[kx, le], 1, cb).astype(BF)
            outs[e, :, theirs] = mm(h[le], other[kx, le], 1, cb).astype(BF)
    row = lax.broadcasted_iota(jnp.int32, (ZT, SL), 0).astype(F32)
    for s in range(NZ):
        hot = jnp.where(targets[s : s + 1, :] == row, 1.0, 0.0).astype(BF)
        out[s] = mm(hot, outs[:, s * 16 : (s + 1) * 16, :].reshape(SL, DS)).astype(BF)


def weight_grad_kernel(up, pos, h0, h1, h2, h3, slots, keep, give):
    x, y, c = pos[1], pos[2], pos[3]
    for k, h in enumerate((h0, h1, h2, h3)):
        q = lax.rem(y - k + NY, NY)
        kx = lax.rem(q - x + NX, NX)
        for le in range(EPD):
            for out, half in ((keep, c), (give, 1 - c)):
                rows = slots[q * EPD + le, :, block(half, HS)]
                grad = mm(rows, h[le], 0, 0) if up else mm(h[le], rows, 0, 0)
                out[kx, le] = grad.astype(BF)


def split_kernel(pos, total, s0, s1, s2, s3):
    y = pos[2]
    for k, out in enumerate((s0, s1, s2, s3)):
        out[...] = total[block(lax.rem(y + k, NY), TOK), :]


def finish_kernel(pos, r0, r1, r2, r3, start, out):
    y = pos[2]
    for k, r in enumerate((r0, r1, r2, r3)):
        part = block(lax.rem(y - k + NY, NY), DS)
        out[:, part] = (start[:, part].astype(F32) + r[...].astype(F32)).astype(BF)


def shift(array, axis, size, by):
    return lax.ppermute(array, axis, [(i, (i + by) % size) for i in range(size)])


def everywhere(array, axis, size):
    return [array] + [shift(array, axis, size, k) for k in range(1, size)]


def exchange(arrays, axis, size):
    return [arrays[0]] + [shift(arrays[k], axis, size, k) for k in range(1, size)]


def add(a, b):
    return (a.astype(F32) + b.astype(F32)).astype(BF)


def after(value, *others):
    return lax.optimization_barrier((value, *others))[0]


def gather_z(array):
    return lax.all_gather(array, "z", tiled=False)


def sum_z(array):
    return lax.psum_scatter(array, "z", scatter_dimension=0, tiled=False)


def back_to_tokens(pos, total):
    return exchange(call(split_kernel, pos, [total], [bf(TOK, DS)] * NY), "y", NY)


def spread_weights(piece):
    own = jnp.stack(everywhere(piece, "x", NX))
    return own, shift(own, "c", NC, 1)


def weight_grad_parts(up, pos, mids, slots):
    tail = (HS, F) if up else (F, HS)
    return call(
        functools.partial(weight_grad_kernel, up),
        pos,
        [*mids, slots],
        [bf(NX, EPD, *tail)] * 2,
        flops=7_000_000_000,
    )


def weight_grad(keep, give, others=()):
    total = after(add(keep, shift(give, "c", NC, 1)), *others)
    return total, exchange([total[k] for k in range(NX)], "x", NX)


def total_of(arrays):
    return functools.reduce(lambda a, b: a + b, [a.astype(F32) for a in arrays]).astype(BF)


def per_device(tokens, routes, gates, cotangent, w_up, w_down):
    z, x, y, c = (lax.axis_index(name) for name in ("z", "x", "y", "c"))
    pos = jnp.stack([z, x, y, c]).astype(jnp.int32)
    sends = call(
        pack_kernel,
        pos,
        [routes.T, gates.T, tokens, cotangent],
        [bf(TOK + TAB, DS)] * NY + [bf(TOK, DS)] * NY,
        flops=4_000_000_000,
    )
    relaid = exchange(sends[:NY], "y", NY)
    start = call(merge_kernel, pos, relaid, bf(ZT + TAB, DS))
    rows = gather_z(start)
    relaid = exchange(after(list(sends[NY:]), start), "y", NY)
    grad_start = call(merge_plain_kernel, pos, relaid, bf(ZT, DS))
    grads_in = gather_z(grad_start)

    at = y * NC + c
    up = spread_weights(after(lax.dynamic_slice_in_dim(w_up, at * HS, HS, 1), grad_start))
    down = everywhere(after(lax.dynamic_slice_in_dim(w_down, at * HS, HS, 2), grad_start), "x", NX)
    rows = after(rows, *up)

    part = [bf(EPD, ROWS, F)] * NY
    slots, p0, p1, p2, p3, gate, targets, hots = call(
        token_kernel,
        pos,
        [rows, *up],
        [bf(EZ, ROWS, DS), *part, f32(EPD, ROWS, F), f32(NZ, SL), bf(NZ, SL, ZT)],
        flops=13_000_000_000,
    )
    down = jnp.stack(after(down, p0))
    down = (down, shift(down, "c", NC, 1))
    pre = exchange([p0, p1, p2, p3], "y", NY)
    hidden, slope = call(hidden_kernel, pos, [*pre, gate], [bf(EPD, ROWS, F), f32(EPD, ROWS, F)])
    hidden = everywhere(hidden, "y", NY)
    outs = bf(NZ, ZT, DS)
    work = [VM((EZ, ROWS, DS), BF)]
    mixed = call(
        functools.partial(combine_kernel, False), pos, [*hidden, targets, *down], outs, work, flops=8_000_000_000
    )
    grad_slots, p0, p1, p2, p3 = call(
        cotangent_kernel,
        pos,
        [after(grads_in, mixed), hots, *down],
        [bf(EZ, ROWS, DS), *part],
        flops=11_000_000_000,
    )
    mixed = sum_z(mixed)
    grads = exchange([p0, p1, p2, p3], "y", NY)
    keep, give = weight_grad_parts(False, pos, hidden, grad_slots)
    grad_pre = everywhere(call(grad_pre_kernel, pos, [*grads, slope], bf(EPD, ROWS, F)), "y", NY)
    down_total, down_parts = weight_grad(keep, give)
    grad_pre = after(grad_pre, keep)
    token_grad = call(
        functools.partial(combine_kernel, True), pos, [*grad_pre, targets, *up], outs, work, flops=8_000_000_000
    )
    keep, give = weight_grad_parts(True, pos, after(grad_pre, token_grad, down_total), slots)
    token_grad = sum_z(token_grad)
    mixed = back_to_tokens(pos, mixed)
    _, up_parts = weight_grad(keep, give, mixed)
    down_grad = total_of(down_parts)
    token_grad = back_to_tokens(pos, after(token_grad, up_parts, down_grad, mixed))
    up_grad = total_of(up_parts)
    mixed = call(finish_kernel, pos, [*mixed, tokens], bf(TOK, D))
    token_grad = call(finish_kernel, pos, [*token_grad, cotangent], bf(TOK, D))
    return mixed, token_grad, up_grad, down_grad


def solution(mesh):
    inner = Mesh(mesh.devices.reshape(NZ, NX, NY, NC), ("z", "x", "y", "c"))
    rows = P(("z", "x", "y", "c"), None)
    experts = P(("z", "x"), None, None)
    return jax.shard_map(
        per_device,
        mesh=inner,
        in_specs=(rows, rows, rows, rows, experts, experts),
        out_specs=(rows, rows, P(("z", "x"), ("y", "c"), None), P(("z", "x"), None, ("y", "c"))),
        check_vma=False,
    )
```
